256 devices in a mesh: tile: 64 (over x_lo, y, z), member: 4 (over x_hi, core).
Axes of the slice: x: 4 (x_hi: 2, x_lo: 2; x = x_hi * 2 + x_lo), y: 4, z: 8, core: 2. Of those that a mesh axis runs over, the one named last changes fastest.
Arguments:
- states: bfloat16 [4, 16384, 512], P('member', 'tile'), may hold values from -105 to 105
- teacher: bfloat16 [16384, 512], P('tile'), may hold values from -6 to 6
- w_qkv: bfloat16 [512, 1536], replicated, may hold values from -0.25 to 0.25
- w_out: bfloat16 [512, 512], replicated, may hold values from -0.25 to 0.25
- gain: float32 [512], replicated, may hold values from 0.1 to 1.9
- bias: float32 [8, 64, 64], replicated, may hold values from -4 to 400
- neighbours: int32 [256, 9], P('tile'), may hold values from 0 to 255, as said below
- valid: int32 [256, 9], P('tile'), may hold values from 0 to 1, as said below
- orient: int32 [256, 9], P('tile'), may hold values from 0 to 3, as said below
Outputs:
- output: bfloat16 [4, 16384, 512], P('member', 'tile')
- d_states: bfloat16 [4, 16384, 512], P('member', 'tile')
- d_wqkv: float32 [512, 1536], P('tile', 'member')
- d_wout: float32 [512, 512], P('tile', 'member')
- d_gain: float32 [512], replicated
- d_bias: float32 [8, 64, 64], replicated
The draws below stay inside these ranges and needn't reach their ends.
Inputs may be any that keep to these rules, and one draw needn't show every extreme that they name: `neighbours`: for a block in column c, slots 3 m, 3 m + 1 and 3 m + 2 name blocks of column c + m - 1, block = column * 4 + row; where c + m - 1 lies outside 0 to 64 - 1 (the window's open ends) these slots name the block itself; slot 4 names the block itself. `valid`: slot 4 is always 1; slots whose column lies outside the window are 0. `orient`: slot 4 is always 0.
All inputs are finite; a program needn't handle non-finite values.
Results may differ from the reference program's by a relative error of at most 0.008.
Values may be sent and summed in bfloat16 or wider, within the bound.
A program may use at most 128 MiB of HBM per device.

```python
import jax
import jax.numpy as jnp
from jax import lax

D = 512
HEADS = 8
HD = 64
SIDE = 8
PIX = 64
ROWS = 4
SLOTS = 9
COLS = 64
BLOCKS = 256
PIXELS = 16384
MEMBERS = 4


def draw_states(key, part):
    keys = jax.random.split(key, 3)
    base = jnp.clip(jax.random.normal(keys[0], (MEMBERS, PIXELS, D), jnp.float32), -6.0, 6.0)
    row_scale = jnp.exp(jax.random.uniform(keys[1], (MEMBERS, PIXELS, 1), jnp.float32, -1.15, 1.15))
    column_scale = jnp.exp(jax.random.uniform(keys[2], (1, 1, D), jnp.float32, -1.15, 1.15))
    rising = jnp.exp(jnp.log(3.0) * (jnp.arange(PIXELS, dtype=jnp.float32) / PIXELS - 0.5))[None, :, None]
    return (base * row_scale * column_scale * rising).astype(jnp.bfloat16)


def draw_bias(key, part):
    base = jnp.clip(jax.random.normal(key, (HEADS, PIX, PIX), jnp.float32), -4.0, 4.0)
    return base


def outside_window():
    blocks = jnp.arange(BLOCKS, dtype=jnp.int32)[:, None]
    slots = jnp.arange(SLOTS, dtype=jnp.int32)[None, :]
    column = blocks // ROWS + slots // 3 - 1
    return (column < 0) | (column >= COLS)


def draw_neighbours(key, part):
    blocks = jnp.arange(BLOCKS, dtype=jnp.int32)[:, None]
    slots = jnp.arange(SLOTS, dtype=jnp.int32)[None, :]
    row_pick = jax.random.randint(key, (BLOCKS, SLOTS), 0, ROWS, dtype=jnp.int32)
    column = blocks // ROWS + slots // 3 - 1
    named = column * ROWS + row_pick
    return jnp.where((slots == 4) | outside_window(), blocks, named).astype(jnp.int32)


def draw_valid(key, part):
    slots = jnp.arange(SLOTS, dtype=jnp.int32)[None, :]
    pick = jax.random.randint(jax.random.fold_in(key, 11), (BLOCKS, SLOTS), 0, 4, dtype=jnp.int32)
    kept = jnp.where(outside_window(), 0, jnp.where(pick > 0, 1, 0))
    return jnp.where(slots == 4, 1, kept).astype(jnp.int32)


def draw_orient(key, part):
    slots = jnp.arange(SLOTS, dtype=jnp.int32)[None, :]
    pick = jax.random.randint(jax.random.fold_in(key, 23), (BLOCKS, SLOTS), 0, 4, dtype=jnp.int32)
    return jnp.where(slots == 4, 0, pick).astype(jnp.int32)


def levels(stream_key, shape, pieces, low, largest):
    level = 1.0
    for dim, shards_of in pieces:
        draws = jax.random.uniform(jax.random.fold_in(jax.random.fold_in(stream_key, 6), dim), (shards_of,), jnp.float32, low / len(pieces), largest / len(pieces))
        level = level * jnp.repeat(jnp.exp(draws), shape[dim] // shards_of).reshape((-1,) + (1,) * (len(shape) - 1 - dim))
    return level


def scatter_about(key, dims, spread, limit, cuts=(), kind=jnp.bfloat16):
    array = spread * jax.random.normal(key, dims, jnp.float32)
    if cuts:
        array = array * levels(key, dims, cuts, -0.22, 0.18)
    return jnp.clip(array, -limit, limit).astype(kind)


def setup_inputs(seed: int = 0) -> dict:
    key_list = jax.random.split(jax.random.key(seed), 10)
    states = draw_states(jax.random.fold_in(key_list[9], 71), 0)
    teacher = scatter_about(key_list[1], (PIXELS, D), 1.0, 6.0, ((0, 64),))
    w_qkv = scatter_about(key_list[2], (D, 3 * D), D ** -0.5, 0.25)
    w_out = scatter_about(key_list[3], (D, D), D ** -0.5, 0.25)
    gain = jnp.clip(1.0 + 0.18 * jax.random.normal(key_list[4], (D,), jnp.float32), 0.1, 1.9)
    bias = draw_bias(jax.random.fold_in(key_list[9], 71), 0)
    neighbours = draw_neighbours(jax.random.fold_in(key_list[9], 71), 0)
    valid = draw_valid(jax.random.fold_in(key_list[9], 71), 0)
    orient = draw_orient(jax.random.fold_in(key_list[9], 71), 0)
    return {"states": states, "teacher": teacher, "w_qkv": w_qkv, "w_out": w_out, "gain": gain, "bias": bias, "neighbours": neighbours, "valid": valid, "orient": orient}


EPS = 1e-06
NEG = -1e+30
HIGH = lax.Precision.HIGHEST

def turn_onehot():
    position = jnp.arange(PIX, dtype=jnp.int32)
    upper = position // SIDE
    lower = position % SIDE
    tables = []
    for turn in range(4):
        tables.append(upper * SIDE + lower)
        upper, lower = (lower, SIDE - 1 - upper)
    table = jnp.stack(tables)
    return (table[:, :, None] == position[None, None, :]).astype(jnp.float32)

def probabilities(queries, keys_near, alive, turn_pick, turned):
    scores = jnp.einsum('gihd,gsjhd->ghisj', queries.astype(jnp.float32), keys_near.astype(jnp.float32)) * HD ** (-0.5)
    scores = scores + jnp.einsum('gsk,khij->ghisj', turn_pick, turned, precision=HIGH)
    inside = alive[:, None, None, :, None]
    masked = jnp.where(inside, scores, NEG)
    highest = lax.optimization_barrier(jnp.max(masked, axis=(3, 4), keepdims=True))
    weights = jnp.where(inside, jnp.exp(masked - highest), 0.0)
    return weights / lax.optimization_barrier(jnp.sum(weights, axis=(3, 4), keepdims=True))

def member_pass(inputs, teacher, w_qkv, w_out, gain, turned, near_cols, alive_cols, pick_cols):
    inputs32 = inputs.astype(jnp.float32)
    inverse = lax.rsqrt(lax.optimization_barrier(jnp.mean(inputs32 * inputs32, axis=-1, keepdims=True)) + EPS)
    normed = (inputs32 * inverse * gain).astype(jnp.bfloat16)
    projected = jnp.dot(normed, w_qkv, preferred_element_type=jnp.float32).astype(jnp.bfloat16)
    queries = projected[:, :D].reshape(COLS, ROWS, PIX, HEADS, HD)
    keys_all = projected[:, D:2 * D].reshape(BLOCKS, PIX, HEADS, HD)
    values_all = projected[:, 2 * D:].reshape(BLOCKS, PIX, HEADS, HD)

    def forward_column(packed):
        query_col, near_col, alive_col, pick_col = packed
        keys_near = keys_all[near_col]
        values_near = values_all[near_col]
        probs = probabilities(query_col, keys_near, alive_col, pick_col, turned)
        probs_low = probs.astype(jnp.bfloat16)
        return jnp.einsum('ghisj,gsjhd->gihd', probs_low.astype(jnp.float32), values_near.astype(jnp.float32)).astype(jnp.bfloat16)
    mixed = lax.map(forward_column, (queries, near_cols, alive_cols, pick_cols)).reshape(PIXELS, D)
    output32 = inputs32 + jnp.dot(mixed, w_out, preferred_element_type=jnp.float32)
    d_output = (output32 - teacher.astype(jnp.float32)).astype(jnp.bfloat16)
    d_mixed = jnp.dot(d_output, w_out.T, preferred_element_type=jnp.float32).astype(jnp.bfloat16)
    d_mixed = d_mixed.reshape(COLS, ROWS, PIX, HEADS, HD)

    def backward_column(carry, packed):
        d_keyval, d_turned = carry
        query_col, dmix_col, near_col, alive_col, pick_col = packed
        keys_near = keys_all[near_col]
        values_near = values_all[near_col]
        probs = probabilities(query_col, keys_near, alive_col, pick_col, turned)
        probs_low = probs.astype(jnp.bfloat16)
        d_probs = jnp.einsum('gihd,gsjhd->ghisj', dmix_col.astype(jnp.float32), values_near.astype(jnp.float32))
        delta_sum = lax.optimization_barrier(jnp.sum(probs * d_probs, axis=(3, 4), keepdims=True))
        d_scores = probs * (d_probs - delta_sum)
        d_scores_low = d_scores.astype(jnp.bfloat16).astype(jnp.float32)
        d_queries = (jnp.einsum('ghisj,gsjhd->gihd', d_scores_low, keys_near.astype(jnp.float32)) * HD ** (-0.5)).astype(jnp.bfloat16)
        d_keys = jnp.einsum('ghisj,gihd->gsjhd', d_scores_low, query_col.astype(jnp.float32)) * HD ** (-0.5)
        d_values = jnp.einsum('ghisj,gihd->gsjhd', probs_low.astype(jnp.float32), dmix_col.astype(jnp.float32))
        both = jnp.concatenate([d_keys.reshape(ROWS * SLOTS, PIX, D), d_values.reshape(ROWS * SLOTS, PIX, D)], axis=-1)
        d_keyval = d_keyval.at[near_col.reshape(-1)].add(both)
        d_turned = d_turned + jnp.einsum('gsk,ghisj->khij', pick_col, d_scores, precision=HIGH)
        return ((d_keyval, d_turned), d_queries)
    start_carry = (jnp.zeros((BLOCKS, PIX, 2 * D), jnp.float32), jnp.zeros((4, HEADS, PIX, PIX), jnp.float32))
    (d_keyval, d_turned), d_queries = lax.scan(backward_column, start_carry, (queries, d_mixed, near_cols, alive_cols, pick_cols))
    d_proj = jnp.concatenate([d_queries.reshape(PIXELS, D), d_keyval.reshape(PIXELS, 2 * D).astype(jnp.bfloat16)], axis=-1)
    d_normed = jnp.dot(d_proj, w_qkv.T, preferred_element_type=jnp.float32)
    d_gain = lax.optimization_barrier(jnp.sum(d_normed * inputs32 * inverse, axis=0))
    d_scaled = d_normed * gain
    d_inputs = d_output.astype(jnp.float32) + inverse * d_scaled - inputs32 * inverse * inverse * inverse * lax.optimization_barrier(jnp.mean(d_scaled * inputs32, axis=-1, keepdims=True))
    d_wqkv = jnp.dot(normed.T, d_proj, preferred_element_type=jnp.float32)
    d_wout = jnp.dot(mixed.T, d_output, preferred_element_type=jnp.float32)
    return (output32.astype(jnp.bfloat16), d_inputs.astype(jnp.bfloat16), d_wqkv, d_wout, d_gain, d_turned)

def reference(states, teacher, w_qkv, w_out, gain, bias, neighbours, valid, orient):
    onehot_turn = turn_onehot()
    turned = jnp.einsum('ail,kjl->kaij', bias, onehot_turn, precision=HIGH)
    near_cols = neighbours.reshape(COLS, ROWS, SLOTS)
    alive_cols = (valid > 0).reshape(COLS, ROWS, SLOTS)
    pick_cols = (orient[:, :, None] == jnp.arange(4, dtype=jnp.int32)[None, None, :]).astype(jnp.float32).reshape(COLS, ROWS, SLOTS, 4)

    def one_member(inputs):
        return member_pass(inputs, teacher, w_qkv, w_out, gain, turned, near_cols, alive_cols, pick_cols)
    output, d_states, d_wqkv, d_wout, d_gain, d_turned = lax.map(one_member, states)
    d_bias = jnp.einsum('khij,kjl->hil', lax.optimization_barrier(jnp.sum(d_turned, axis=0)), onehot_turn, precision=HIGH)
    return (output, d_states, lax.optimization_barrier(jnp.sum(d_wqkv, axis=0)), lax.optimization_barrier(jnp.sum(d_wout, axis=0)), lax.optimization_barrier(jnp.sum(d_gain, axis=0)), d_bias)
```

```python
import functools

import jax
import jax.numpy as jnp
from jax import lax
from jax.experimental import pallas as pl
from jax.experimental.pallas import tpu as pltpu
from jax.sharding import PartitionSpec as P

D = 512
HEADS = 8
HD = 64
PIX = 64
ROWS = 4
SLOTS = 9
HALF = 256
EPS = 1e-06
NEG = -1e30
MESH = pl.DeviceIdType.MESH
F32 = jnp.float32
BF16 = jnp.bfloat16

NX, NY, NZ, NXL = 4, 4, 8, 2
N_TILE = NXL * NY * NZ

NN = (((1,), (0,)), ((), ()))
NT = (((1,), (1,)), ((), ()))
TN = (((0,), (0,)), ((), ()))


def mm(a, b, dims=NN):
    return lax.dot_general(a, b, dims, preferred_element_type=F32)


def kernel(
    x_ref, teacher_ref, wqkv_ref, wout_ref, gain_ref, bias_ref, near_ref, valid_ref, orient_ref,
    out_ref, dst_ref, dwqkv_ref, dwout_ref, dgain_ref, dbias_ref,
    xh, nb, kbuf, vbuf, tb, oh, qb, kg, vg, sref, pb, rinv, mixed, dmix, dout, dsb, dq,
    qd, md, dcat, pcat, dkv, esend, erecv, turns,
    g0, r0, s1, ra1, rb1, a1, b1, ra2, rb2, c3, rz,
    u0, ruz, w0, ruc, rux, ruy, fz,
    send, recv,
):
    tile = lax.axis_index("tile")
    member = lax.axis_index("member")
    z = lax.rem(tile, NZ)
    y = lax.rem(tile // NZ, NY)
    x = (member // 2) * NXL + tile // (NZ * NY)
    core = lax.rem(member, 2)

    def at(x_=None, y_=None, z_=None, core_=None):
        x_ = x if x_ is None else x_
        y_ = y if y_ is None else y_
        z_ = z if z_ is None else z_
        core_ = core if core_ is None else core_
        return (lax.rem(x_, NXL) * NY + y_) * NZ + z_, (x_ // NXL) * 2 + core_

    right = (lax.rem(tile + 1, N_TILE), member)
    left = (lax.rem(tile + N_TILE - 1, N_TILE), member)
    sibling = at(core_=1 - core)
    xs = [lax.rem(x + o, NX) for o in range(1, NX)]
    ys = [lax.rem(y + o, NY) for o in range(1, NY)]
    zs = [lax.rem(z + o, NZ) for o in range(1, NZ)]
    peers = [left, right, sibling]
    peers += [at(x_=v) for v in xs] + [at(y_=v) for v in ys] + [at(z_=v) for v in zs]

    started = []

    def push(src, dst, to):
        n = len(started)
        copy = pltpu.make_async_remote_copy(
            src_ref=src, dst_ref=dst, send_sem=send.at[n], recv_sem=recv.at[n],
            device_id=to, device_id_type=MESH,
        )
        copy.start()
        started.append(copy)
        return copy

    barrier = pltpu.get_barrier_semaphore()
    for p in peers:
        pl.semaphore_signal(barrier, inc=1, device_id=p, device_id_type=MESH)
    pl.semaphore_wait(barrier, len(peers))

    to_right = push(x_ref, xh.at[0], right)
    to_left = push(x_ref, xh.at[1], left)

    gain = gain_ref[...]

    def inverse_of(v32):
        return lax.rsqrt(jnp.mean(v32 * v32, axis=-1, keepdims=True) + EPS)

    def normalised(v):
        v32 = v.astype(F32)
        return (v32 * inverse_of(v32) * gain).astype(BF16)

    nb[HALF:2 * HALF, :] = normalised(x_ref[...])
    own = nb[HALF:2 * HALF, :]
    qb[...] = (mm(own, wqkv_ref[:, :D]).astype(BF16) * 0.125).astype(BF16)

    def keys_values(m):
        rows = nb[m * HALF:(m + 1) * HALF, :]
        kbuf[m * ROWS:(m + 1) * ROWS] = mm(rows, wqkv_ref[:, D:2 * D]).astype(BF16).reshape(ROWS, PIX, D)
        vbuf[m * ROWS:(m + 1) * ROWS] = mm(rows, wqkv_ref[:, 2 * D:]).astype(BF16).reshape(ROWS, PIX, D)

    keys_values(1)

    j = lax.broadcasted_iota(jnp.int32, (PIX, 128), 0)
    l = lax.broadcasted_iota(jnp.int32, (PIX, 128), 1)
    u, w = j // 8, j % 8
    for o in range(4):
        oh[o] = jnp.where(l == u * 8 + w, 1.0, 0.0).astype(BF16)
        pick = jnp.where(l[:, :PIX] == (u * 8 + w)[:, :PIX], 1.0, 0.0)
        tb[o] = lax.dot_general(
            pick, bias_ref[...], NT, precision=lax.Precision.HIGHEST, preferred_element_type=F32
        )
        u, w = w, 7 - u
    tb[4] = jnp.full((PIX, D), NEG, F32)

    head_row = lax.broadcasted_iota(jnp.int32, (HALF, HALF), 0) // HD
    head_lane = lax.broadcasted_iota(jnp.int32, (HALF, HALF), 1) // HD
    same_head = jnp.where(head_row == head_lane, 1.0, 0.0).astype(BF16)
    lane_head = lax.broadcasted_iota(jnp.int32, (PIX, HALF), 1) // HD

    def block_diagonal(v):
        return jnp.concatenate([v] * 4, axis=0) * same_head

    def diagonal(v):
        out = v[:PIX]
        for a in range(1, 4):
            out = jnp.where(lane_head == a, v[a * PIX:(a + 1) * PIX], out)
        return out

    groups = [slice(0, HALF), slice(HALF, D)]

    to_right.wait_recv()
    to_left.wait_recv()
    nb[:HALF, :] = normalised(xh[0])
    nb[2 * HALF:, :] = normalised(xh[1])
    keys_values(0)
    keys_values(2)

    for b in range(ROWS):
        for s in range(SLOTS):
            at_block = (s // 3) * ROWS + lax.rem(near_ref[b, s], ROWS)
            kg[b, s * PIX:(s + 1) * PIX, :] = kbuf[at_block]
            vg[b, s * PIX:(s + 1) * PIX, :] = vbuf[at_block]
        tables = [jnp.where(valid_ref[b, s] > 0, orient_ref[b, s], 4) for s in range(SLOTS)]
        for g, lanes in enumerate(groups):
            diag = block_diagonal(qb[b * PIX:(b + 1) * PIX, lanes])
            qd[g, b * HALF:(b + 1) * HALF, :] = diag
            scores = mm(kg[b, :, lanes], diag, NT)
            top = None
            for s in range(SLOTS):
                piece = scores[s * PIX:(s + 1) * PIX] + tb[tables[s], :, lanes]
                sref[b, s * PIX:(s + 1) * PIX, lanes] = piece
                top = piece if top is None else jnp.maximum(top, piece)
            top = jnp.max(top, axis=0, keepdims=True)
            total = None
            for s in range(SLOTS):
                piece = jnp.exp(sref[b, s * PIX:(s + 1) * PIX, lanes] - top)
                sref[b, s * PIX:(s + 1) * PIX, lanes] = piece
                total = piece if total is None else total + piece
            share = 1.0 / jnp.sum(total, axis=0, keepdims=True)
            rinv[b, :, lanes] = share
            for s in range(SLOTS):
                piece = sref[b, s * PIX:(s + 1) * PIX, lanes] * share
                pb[b, s, :, lanes] = piece.astype(BF16)
            probs = pb[b, 0:SLOTS, :, lanes].reshape(SLOTS * PIX, HALF)
            mixed[b * PIX:(b + 1) * PIX, lanes] = diagonal(mm(probs, vg[b, :, lanes], TN)).astype(BF16)
        pb[b, SLOTS] = jnp.zeros((PIX, D), BF16)
        dsb[b, SLOTS] = jnp.zeros((PIX, D), BF16)

    out32 = x_ref[...].astype(F32) + mm(mixed[...], wout_ref[...])
    out_ref[...] = out32.astype(BF16)
    dout[...] = (out32 - teacher_ref[...].astype(F32)).astype(BF16)
    dmix[...] = mm(dout[...], wout_ref[...], NT).astype(BF16)

    for b in range(ROWS):
        for g, lanes in enumerate(groups):
            diag = block_diagonal(dmix[b * PIX:(b + 1) * PIX, lanes])
            md[g, b * HALF:(b + 1) * HALF, :] = diag
            dprobs = mm(vg[b, :, lanes], diag, NT)
            share = rinv[b, :, lanes]
            total = None
            for s in range(SLOTS):
                piece = sref[b, s * PIX:(s + 1) * PIX, lanes] * dprobs[s * PIX:(s + 1) * PIX]
                total = piece if total is None else total + piece
            delta = jnp.sum(total, axis=0, keepdims=True) * share
            for s in range(SLOTS):
                piece = sref[b, s * PIX:(s + 1) * PIX, lanes] * share
                piece = piece * (dprobs[s * PIX:(s + 1) * PIX] - delta)
                dsb[b, s, :, lanes] = piece.astype(BF16)
            dscores = dsb[b, 0:SLOTS, :, lanes].reshape(SLOTS * PIX, HALF)
            dq[b * PIX:(b + 1) * PIX, lanes] = (diagonal(mm(dscores, kg[b, :, lanes], TN)) * 0.125).astype(BF16)
        rows = [lax.rem(near_ref[b, s], ROWS) for s in range(SLOTS)]
        for m in range(3):
            for t in range(ROWS):
                slots = [jnp.where(rows[3 * m + k] == t, 3 * m + k, SLOTS) for k in range(3)]
                here = slice((m * ROWS + t) * PIX, (m * ROWS + t + 1) * PIX)
                ds = dsb[b, slots[0]] + dsb[b, slots[1]] + dsb[b, slots[2]]
                ps = pb[b, slots[0]] + pb[b, slots[1]] + pb[b, slots[2]]
                for g, lanes in enumerate(groups):
                    dcat[g, here, b * HALF:(b + 1) * HALF] = ds[:, lanes]
                    pcat[g, here, b * HALF:(b + 1) * HALF] = ps[:, lanes]

    for g in range(2):
        dkv[:, g * HALF:(g + 1) * HALF] = mm(dcat[g], qd[g]).astype(BF16)
        dkv[:, D + g * HALF:D + (g + 1) * HALF] = mm(pcat[g], md[g]).astype(BF16)

    def share_out(value, m, offset):
        low = value.astype(BF16)
        for xl in range(NXL):
            for yy in range(NY):
                for zh in range(2):
                    fb = (xl * NY + yy) * 2 + zh
                    g0[m % 2, zh, (m // 2) * NXL + xl, yy, :, offset:offset + low.shape[1]] = low[fb * 32:(fb + 1) * 32]

    for m in range(4):
        for lo in range(m * 384, m * 384 + 384, 128):
            if lo < D:
                value = mm(own, dq[:, lo:lo + 128], TN)
            else:
                value = mm(nb[...], dkv[:, lo - D:lo - D + 128], TN)
            share_out(value, m, lo - m * 384)
        share_out(mm(mixed[...], dout[:, m * 128:(m + 1) * 128], TN), m, 384)

    g_core = push(g0.at[1 - core], r0, sibling)

    wkv = wqkv_ref[:, D:]

    def scaled(v):
        v32 = v.astype(F32)
        return v32 * inverse_of(v32)

    def by_eight(v):
        return jnp.sum(v.reshape(HALF // 8, 8, D), axis=0)

    edge = mm(dkv[:HALF, :], wkv, NT)
    esend[0] = edge.astype(BF16)
    e_left = push(esend.at[0], erecv.at[0], left)
    gain8 = by_eight(edge * scaled(xh[0]))
    edge = mm(dkv[2 * HALF:, :], wkv, NT)
    esend[1] = edge.astype(BF16)
    e_right = push(esend.at[1], erecv.at[1], right)
    gain8 = gain8 + by_eight(edge * scaled(xh[1]))
    dnorm = mm(dkv[HALF:2 * HALF, :], wkv, NT) + mm(dq[...], wqkv_ref[:, :D], NT)
    gain8 = gain8 + by_eight(dnorm * scaled(x_ref[...]))

    dbias = None
    for b in range(ROWS):
        for s in range(SLOTS):
            turns[s * PIX:(s + 1) * PIX, :] = oh[orient_ref[b, s]]
        part = mm(turns[...], dsb[b, 0:SLOTS].reshape(SLOTS * PIX, D), TN)[:PIX]
        dbias = part if dbias is None else dbias + part

    for i in range(NZ):
        u0[i, :, :D] = dbias[i * 8:(i + 1) * 8]
        u0[i, :, D:] = gain8[:, i * 128:(i + 1) * 128] if i < 4 else jnp.zeros((8, 128), F32)
    u_z = [push(u0.at[v], ruz.at[o], at(z_=v)) for o, v in enumerate(zs)]

    g_core.wait_recv()
    for zh in range(2):
        for xx in range(NX):
            s1[zh, xx] = (g0[core, zh, xx].astype(F32) + r0[zh, xx].astype(F32)).astype(BF16)
    a_x = [push(s1.at[0, v], ra1.at[o], at(x_=v)) for o, v in enumerate(xs)]
    b_y = [push(s1.at[1, :, v], rb1.at[o], at(y_=v)) for o, v in enumerate(ys)]

    for c in u_z:
        c.wait_recv()
    total = u0[z]
    for o in range(NZ - 1):
        total = total + ruz[o]
    w0[...] = total
    u_core = push(w0, ruc, sibling)
    u_core.wait_recv()
    rux[x] = w0[...] + ruc[...]
    u_x = [push(rux.at[x], rux.at[x], at(x_=v)) for v in xs]

    for c in a_x + b_y:
        c.wait_recv()
    a1[...] = (
        s1[0, x].astype(F32) + ra1[0].astype(F32) + ra1[1].astype(F32) + ra1[2].astype(F32)
    ).astype(BF16)
    for xx in range(NX):
        b1[xx] = (
            s1[1, xx, y].astype(F32) + rb1[0, xx].astype(F32) + rb1[1, xx].astype(F32) + rb1[2, xx].astype(F32)
        ).astype(BF16)
    a_y = [push(a1.at[v], ra2.at[o], at(y_=v)) for o, v in enumerate(ys)]
    b_x = [push(b1.at[v], rb2.at[o], at(x_=v)) for o, v in enumerate(xs)]

    for c in u_x:
        c.wait_recv()
    ruy[y] = rux[0] + rux[1] + rux[2] + rux[3]
    u_y = [push(ruy.at[y], ruy.at[y], at(y_=v)) for v in ys]

    for c in a_y + b_x:
        c.wait_recv()
    ca = a1[y].astype(F32) + ra2[0].astype(F32) + ra2[1].astype(F32) + ra2[2].astype(F32)
    cb = b1[x].astype(F32) + rb2[0].astype(F32) + rb2[1].astype(F32) + rb2[2].astype(F32)
    for i in range(NZ):
        part = (ca if i < 4 else cb)[(i % 4) * 8:(i % 4) * 8 + 8]
        c3[i] = jnp.concatenate([part[:, :HALF], part[:, HALF:]], axis=0).astype(BF16)
    c_z = [push(c3.at[v], rz.at[o], at(z_=v)) for o, v in enumerate(zs)]

    for c in u_y:
        c.wait_recv()
    fz[z] = ruy[0] + ruy[1] + ruy[2] + ruy[3]
    f_z = [push(fz.at[z], fz.at[z], at(z_=v)) for v in zs]

    e_left.wait_recv()
    e_right.wait_recv()
    dnorm = dnorm + erecv[0].astype(F32) + erecv[1].astype(F32)
    x32 = x_ref[...].astype(F32)
    inverse = inverse_of(x32)
    dscaled = dnorm * gain
    dst_ref[...] = (
        dout[...].astype(F32)
        + inverse * dscaled
        - x32 * (inverse * inverse * inverse * jnp.mean(dscaled * x32, axis=-1, keepdims=True))
    ).astype(BF16)

    for c in c_z:
        c.wait_recv()
    final = c3[z].astype(F32)
    for o in range(NZ - 1):
        final = final + rz[o].astype(F32)
    dwqkv_ref[:, :HALF] = final[:8]
    dwqkv_ref[:, HALF:] = final[8:, :128]
    dwout_ref[...] = final[8:, 128:]

    for c in f_z:
        c.wait_recv()
    dbias_ref[...] = fz[:, :, :D].reshape(PIX, D).T
    for i in range(4):
        dgain_ref[:, i * 128:(i + 1) * 128] = jnp.sum(fz[i, :, D:], axis=0, keepdims=True)

    for c in started:
        c.wait_send()


N_COPIES = 2 + 1 + 2 + 7 + 6 + 1 + 3 + 6 + 3 + 7 + 7


def scratch():
    def v(*shape, kind=BF16):
        return pltpu.VMEM(shape, kind)

    return [
        v(2, HALF, D), v(3 * HALF, D), v(12, PIX, D), v(12, PIX, D), v(5, PIX, D, kind=F32), v(4, PIX, 128),
        v(HALF, D), v(ROWS, SLOTS * PIX, D), v(ROWS, SLOTS * PIX, D), v(ROWS, SLOTS * PIX, D, kind=F32),
        v(ROWS, SLOTS + 1, PIX, D), v(ROWS, 1, D, kind=F32), v(HALF, D), v(HALF, D), v(HALF, D),
        v(ROWS, SLOTS + 1, PIX, D), v(HALF, D),
        v(2, ROWS * HALF, HALF), v(2, ROWS * HALF, HALF), v(2, 12 * PIX, ROWS * HALF), v(2, 12 * PIX, ROWS * HALF),
        v(3 * HALF, 2 * D), v(2, HALF, D), v(2, HALF, D), v(SLOTS * PIX, 128),
        v(2, 2, NX, NY, 32, D), v(2, NX, NY, 32, D), v(2, NX, NY, 32, D),
        v(NX - 1, NY, 32, D), v(NY - 1, NX, 32, D), v(NY, 32, D), v(NX, 32, D),
        v(NY - 1, 32, D), v(NX - 1, 32, D), v(NZ, 16, HALF), v(NZ - 1, 16, HALF),
        v(NZ, 8, D + 128, kind=F32), v(NZ - 1, 8, D + 128, kind=F32), v(8, D + 128, kind=F32), v(8, D + 128, kind=F32),
        v(NX, 8, D + 128, kind=F32), v(NY, 8, D + 128, kind=F32), v(NZ, 8, D + 128, kind=F32),
        pltpu.SemaphoreType.DMA((N_COPIES,)), pltpu.SemaphoreType.DMA((N_COPIES,)),
    ]


def shards(states, teacher, w_qkv, w_out, gain, bias, neighbours, valid, orient):
    vmem = pl.BlockSpec(memory_space=pltpu.VMEM)
    smem = pl.BlockSpec(memory_space=pltpu.SMEM)
    output, d_states, d_wqkv, d_wout, d_gain, d_bias = pl.pallas_call(
        kernel,
        out_shape=[
            jax.ShapeDtypeStruct((HALF, D), BF16),
            jax.ShapeDtypeStruct((HALF, D), BF16),
            jax.ShapeDtypeStruct((8, 384), F32),
            jax.ShapeDtypeStruct((8, 128), F32),
            jax.ShapeDtypeStruct((1, D), F32),
            jax.ShapeDtypeStruct((HEADS * PIX, PIX), F32),
        ],
        in_specs=[vmem] * 6 + [smem] * 3,
        out_specs=[vmem] * 6,
        scratch_shapes=scratch(),
        compiler_params=pltpu.CompilerParams(
            collective_id=0, has_side_effects=True, vmem_limit_bytes=60 * 2**20
        ),
    )(
        states[0], teacher, w_qkv, w_out, gain.reshape(1, D), bias.reshape(HEADS * PIX, PIX),
        neighbours, valid, orient,
    )
    return output[None], d_states[None], d_wqkv, d_wout, d_gain[0], d_bias.reshape(HEADS, PIX, PIX)


def solution(mesh):
    return jax.shard_map(
        shards,
        mesh=mesh,
        in_specs=(
            P("member", "tile", None), P("tile", None), P(), P(), P(), P(),
            P("tile", None), P("tile", None), P("tile", None),
        ),
        out_specs=(
            P("member", "tile", None), P("member", "tile", None), P("tile", "member"), P("tile", "member"), P(), P(),
        ),
        check_vma=False,
    )
```

```python
import functools

import jax
import jax.numpy as jnp
from jax import lax
from jax.experimental import pallas as pl
from jax.experimental.pallas import tpu as pltpu
from jax.sharding import PartitionSpec as P

D = 512
HEADS = 8
HD = 64
PIX = 64
ROWS = 4
SLOTS = 9
HALF = 256
EPS = 1e-06
NEG = -1e30
MESH = pl.DeviceIdType.MESH
F32 = jnp.float32
BF16 = jnp.bfloat16

NX, NY, NZ, NXL = 4, 4, 8, 2
N_TILE = NXL * NY * NZ

NN = (((1,), (0,)), ((), ()))
NT = (((1,), (1,)), ((), ()))
TN = (((0,), (0,)), ((), ()))


def mm(a, b, dims=NN):
    return lax.dot_general(a, b, dims, preferred_element_type=F32)


def kernel(
    x_hbm, teacher_hbm, wqkv_hbm, wout_hbm, gain_ref, bias_hbm, near_ref, valid_ref, orient_ref,
    out_hbm, dst_hbm, dwqkv_ref, dwout_ref, dgain_ref, dbias_ref,
    x_ref, teacher_ref, wqkv_ref, wout_ref, bias_ref, out_ref, dst_ref,
    xh, nb, nbt, kbuf, vbuf, tb, oh, qb, kg, vg, sref, pb, rinv, mixed, dmix, dout, dsb, dproj,
    qd, md, dcat, pcat, esend, erecv, turns,
    ga, ra, sa, ga1, ha1, ga2, ha2, ga3, ha3, ga4, ra4,
    gb, rb, sb, gb1, hb1, gb2, hb2, gb3, hb3, gb4, rb4,
    u0, ruz, w0, ruc, rux, ruy, fz, v0, vc, vx, vy, vz,
    send, recv, local,
):
    tile = lax.axis_index("tile")
    member = lax.axis_index("member")
    z = lax.rem(tile, NZ)
    y = lax.rem(tile // NZ, NY)
    x = (member // 2) * NXL + tile // (NZ * NY)
    core = lax.rem(member, 2)

    def at(x_=None, y_=None, z_=None, core_=None):
        x_ = x if x_ is None else x_
        y_ = y if y_ is None else y_
        z_ = z if z_ is None else z_
        core_ = core if core_ is None else core_
        return (lax.rem(x_, NXL) * NY + y_) * NZ + z_, (x_ // NXL) * 2 + core_

    right = (lax.rem(tile + 1, N_TILE), member)
    left = (lax.rem(tile + N_TILE - 1, N_TILE), member)
    sibling = at(core_=1 - core)
    xs = [lax.rem(x + o, NX) for o in range(1, NX)]
    ys = [lax.rem(y + o, NY) for o in range(1, NY)]
    zs = [lax.rem(z + o, NZ) for o in range(1, NZ)]
    peers = [left, right, sibling]
    peers += [at(x_=v) for v in xs] + [at(y_=v) for v in ys] + [at(z_=v) for v in zs]

    started = []
    moves = []

    def push(src, dst, to):
        n = len(started)
        copy = pltpu.make_async_remote_copy(
            src_ref=src, dst_ref=dst, send_sem=send.at[n], recv_sem=recv.at[n],
            device_id=to, device_id_type=MESH,
        )
        copy.start()
        started.append(copy)
        return copy

    def move(src, dst):
        copy = pltpu.make_async_copy(src, dst, local.at[len(moves)])
        copy.start()
        moves.append(copy)
        return copy

    def arrived(copies):
        for c in copies:
            c.wait_recv()

    barrier = pltpu.get_barrier_semaphore()
    for p in peers:
        pl.semaphore_signal(barrier, inc=1, device_id=p, device_id_type=MESH)
    load_x = move(x_hbm, x_ref)
    load_qkv = move(wqkv_hbm, wqkv_ref)
    load_bias = move(bias_hbm, bias_ref)
    load_out = move(wout_hbm, wout_ref)
    load_teacher = move(teacher_hbm, teacher_ref)
    pl.semaphore_wait(barrier, len(peers))

    states_moves = [push(x_hbm, xh.at[0], right), push(x_hbm, xh.at[1], left)]

    gain = gain_ref[...]

    def inverse_of(v32):
        return lax.rsqrt(jnp.mean(v32 * v32, axis=-1, keepdims=True) + EPS)

    def normalise(m, v):
        v32 = v.astype(F32)
        low = (v32 * inverse_of(v32) * gain).astype(BF16)
        nb[m * HALF:(m + 1) * HALF, :] = low
        nbt[:, m * HALF:(m + 1) * HALF] = low.T

    load_x.wait()
    normalise(1, x_ref[...])
    own = nb[HALF:2 * HALF, :]
    load_qkv.wait()
    qb[...] = (mm(own, wqkv_ref[:, :D]).astype(BF16) * 0.125).astype(BF16)

    def keys_values(m):
        rows = nb[m * HALF:(m + 1) * HALF, :]
        kbuf[m * ROWS:(m + 1) * ROWS] = mm(rows, wqkv_ref[:, D:2 * D]).astype(BF16).reshape(ROWS, PIX, D)
        vbuf[m * ROWS:(m + 1) * ROWS] = mm(rows, wqkv_ref[:, 2 * D:]).astype(BF16).reshape(ROWS, PIX, D)

    keys_values(1)

    load_bias.wait()
    j = lax.broadcasted_iota(jnp.int32, (PIX, 128), 0)
    l = lax.broadcasted_iota(jnp.int32, (PIX, 128), 1)
    u, w = j // 8, j % 8
    for o in range(4):
        oh[o] = jnp.where(l == u * 8 + w, 1.0, 0.0).astype(BF16)
        pick = jnp.where(l[:, :PIX] == (u * 8 + w)[:, :PIX], 1.0, 0.0)
        tb[o] = lax.dot_general(
            pick, bias_ref[...], NT, precision=lax.Precision.HIGHEST, preferred_element_type=F32
        )
        u, w = w, 7 - u
    tb[4] = jnp.full((PIX, D), NEG, F32)

    head_row = lax.broadcasted_iota(jnp.int32, (HALF, HALF), 0) // HD
    head_lane = lax.broadcasted_iota(jnp.int32, (HALF, HALF), 1) // HD
    same_head = jnp.where(head_row == head_lane, 1.0, 0.0).astype(BF16)
    lane_head = lax.broadcasted_iota(jnp.int32, (PIX, HALF), 1) // HD

    def block_diagonal(v):
        return jnp.concatenate([v] * 4, axis=0) * same_head

    def diagonal(v):
        out = v[:PIX]
        for a in range(1, 4):
            out = jnp.where(lane_head == a, v[a * PIX:(a + 1) * PIX], out)
        return out

    groups = [slice(0, HALF), slice(HALF, D)]
    tables = [[jnp.where(valid_ref[b, s] > 0, orient_ref[b, s], 4) for s in range(SLOTS)] for b in range(ROWS)]

    def score(b, slots):
        for s in slots:
            at_block = (s // 3) * ROWS + lax.rem(near_ref[b, s], ROWS)
            kg[b, s * PIX:(s + 1) * PIX, :] = kbuf[at_block]
            vg[b, s * PIX:(s + 1) * PIX, :] = vbuf[at_block]
        first, n = slots[0], len(slots)
        for g, lanes in enumerate(groups):
            scores = mm(kg[b, first * PIX:(first + n) * PIX, lanes], qd[g, b * HALF:(b + 1) * HALF, :], NT)
            for i, s in enumerate(slots):
                sref[b, s * PIX:(s + 1) * PIX, lanes] = scores[i * PIX:(i + 1) * PIX] + tb[tables[b][s], :, lanes]

    for b in range(ROWS):
        for g, lanes in enumerate(groups):
            qd[g, b * HALF:(b + 1) * HALF, :] = block_diagonal(qb[b * PIX:(b + 1) * PIX, lanes])
        score(b, (3, 4, 5))
        pb[b, SLOTS] = jnp.zeros((PIX, D), BF16)
        dsb[b, SLOTS] = jnp.zeros((PIX, D), BF16)
    dproj[:HALF, :D] = jnp.zeros((HALF, D), BF16)
    dproj[2 * HALF:, :D] = jnp.zeros((HALF, D), BF16)

    arrived(states_moves)
    normalise(0, xh[0])
    keys_values(0)
    normalise(2, xh[1])
    keys_values(2)

    for b in range(ROWS):
        score(b, (0, 1, 2))
        score(b, (6, 7, 8))
        for g, lanes in enumerate(groups):
            top = None
            for s in range(SLOTS):
                piece = sref[b, s * PIX:(s + 1) * PIX, lanes]
                top = piece if top is None else jnp.maximum(top, piece)
            top = jnp.max(top, axis=0, keepdims=True)
            total = None
            for s in range(SLOTS):
                piece = jnp.exp(sref[b, s * PIX:(s + 1) * PIX, lanes] - top)
                sref[b, s * PIX:(s + 1) * PIX, lanes] = piece
                total = piece if total is None else total + piece
            share = 1.0 / jnp.sum(total, axis=0, keepdims=True)
            rinv[b, :, lanes] = share
            for s in range(SLOTS):
                piece = sref[b, s * PIX:(s + 1) * PIX, lanes] * share
                pb[b, s, :, lanes] = piece.astype(BF16)
            probs = pb[b, 0:SLOTS, :, lanes].reshape(SLOTS * PIX, HALF)
            mixed[b * PIX:(b + 1) * PIX, lanes] = diagonal(mm(probs, vg[b, :, lanes], TN)).astype(BF16)

    load_out.wait()
    load_teacher.wait()
    out32 = x_ref[...].astype(F32) + mm(mixed[...], wout_ref[...])
    out_ref[...] = out32.astype(BF16)
    move(out_ref, out_hbm)
    dout[...] = (out32 - teacher_ref[...].astype(F32)).astype(BF16)
    dmix[...] = mm(dout[...], wout_ref[...], NT).astype(BF16)

    def lay_out(grads, c, xh_, value):
        low = value.astype(BF16)
        for xl in range(NXL):
            for yy in range(NY):
                for zh in range(2):
                    fb = (xl * NY + yy) * 2 + zh
                    grads[c, xh_, zh, xl, yy] = low[fb * 32:(fb + 1) * 32]

    def core_sum(grads, got, total):
        for xh_ in range(2):
            for zh in range(2):
                for xl in range(NXL):
                    total[zh, xh_ * NXL + xl] = (
                        grads[core, xh_, zh, xl].astype(F32) + got[xh_, zh, xl].astype(F32)
                    ).astype(BF16)

    def first_hops(total, by_x, by_y):
        copies = [push(total.at[0, v], by_x.at[o], at(x_=v)) for o, v in enumerate(xs)]
        return copies + [push(total.at[1, :, v], by_y.at[o], at(y_=v)) for o, v in enumerate(ys)]

    def first_sums(total, by_x, by_y, one, two):
        one[...] = (
            total[0, x].astype(F32) + by_x[0].astype(F32) + by_x[1].astype(F32) + by_x[2].astype(F32)
        ).astype(BF16)
        for xx in range(NX):
            two[xx] = (
                total[1, xx, y].astype(F32) + by_y[0, xx].astype(F32) + by_y[1, xx].astype(F32)
                + by_y[2, xx].astype(F32)
            ).astype(BF16)

    def second_hops(one, two, by_y, by_x):
        copies = [push(one.at[v], by_y.at[o], at(y_=v)) for o, v in enumerate(ys)]
        return copies + [push(two.at[v], by_x.at[o], at(x_=v)) for o, v in enumerate(xs)]

    def second_sums(one, two, by_y, by_x):
        ca = one[y].astype(F32) + by_y[0].astype(F32) + by_y[1].astype(F32) + by_y[2].astype(F32)
        cb = two[x].astype(F32) + by_x[0].astype(F32) + by_x[1].astype(F32) + by_x[2].astype(F32)
        return [(ca if i < 4 else cb)[(i % 4) * 8:(i % 4) * 8 + 8] for i in range(NZ)]

    grad_out = mm(mixed[...], dout[...], TN)
    for m in range(4):
        lay_out(ga, m % 2, m // 2, grad_out[:, m * 128:(m + 1) * 128])
    a_core = [push(ga.at[1 - core], ra, sibling)]

    dbias = None
    for b in range(ROWS):
        for g, lanes in enumerate(groups):
            diag = block_diagonal(dmix[b * PIX:(b + 1) * PIX, lanes])
            md[g, b * HALF:(b + 1) * HALF, :] = diag
            dprobs = mm(vg[b, :, lanes], diag, NT)
            share = rinv[b, :, lanes]
            total = None
            for s in range(SLOTS):
                piece = sref[b, s * PIX:(s + 1) * PIX, lanes] * dprobs[s * PIX:(s + 1) * PIX]
                total = piece if total is None else total + piece
            delta = jnp.sum(total, axis=0, keepdims=True) * share
            for s in range(SLOTS):
                piece = sref[b, s * PIX:(s + 1) * PIX, lanes] * share
                piece = piece * (dprobs[s * PIX:(s + 1) * PIX] - delta)
                dsb[b, s, :, lanes] = piece.astype(BF16)
            dscores = dsb[b, 0:SLOTS, :, lanes].reshape(SLOTS * PIX, HALF)
            dproj[HALF + b * PIX:HALF + (b + 1) * PIX, lanes] = (
                diagonal(mm(dscores, kg[b, :, lanes], TN)) * 0.125
            ).astype(BF16)
        for s in range(SLOTS):
            turns[s * PIX:(s + 1) * PIX, :] = oh[orient_ref[b, s]]
        term = mm(turns[...], dsb[b, 0:SLOTS].reshape(SLOTS * PIX, D), TN)[:PIX]
        dbias = term if dbias is None else dbias + term

    for i in range(NZ):
        u0[i] = jnp.concatenate(
            [dbias[i * 8:(i + 1) * 8, :HALF], dbias[i * 8:(i + 1) * 8, HALF:]], axis=0
        ).astype(BF16)
    u_z = [push(u0.at[v], ruz.at[o], at(z_=v)) for o, v in enumerate(zs)]

    arrived(a_core)
    core_sum(ga, ra, sa)
    a_first = first_hops(sa, ga1, ha1)

    for b in range(ROWS):
        rows = [lax.rem(near_ref[b, s], ROWS) for s in range(SLOTS)]
        for m in range(3):
            for t in range(ROWS):
                slots = [jnp.where(rows[3 * m + k] == t, 3 * m + k, SLOTS) for k in range(3)]
                here = slice((m * ROWS + t) * PIX, (m * ROWS + t + 1) * PIX)
                ds = dsb[b, slots[0]] + dsb[b, slots[1]] + dsb[b, slots[2]]
                ps = pb[b, slots[0]] + pb[b, slots[1]] + pb[b, slots[2]]
                for g, lanes in enumerate(groups):
                    dcat[g, here, b * HALF:(b + 1) * HALF] = ds[:, lanes]
                    pcat[g, here, b * HALF:(b + 1) * HALF] = ps[:, lanes]
    for g in range(2):
        dproj[:, D + g * HALF:D + (g + 1) * HALF] = mm(dcat[g], qd[g]).astype(BF16)
        dproj[:, 2 * D + g * HALF:2 * D + (g + 1) * HALF] = mm(pcat[g], md[g]).astype(BF16)

    def member_grads(c, xh_):
        lanes = pl.ds(pl.multiple_of((xh_ * 2 + c) * 384, 128), 384)
        lay_out(gb, c, xh_, mm(nbt[...], dproj[:, lanes]))

    b_core = []
    for xh_ in range(2):
        member_grads(1 - core, xh_)
        b_core.append(push(gb.at[1 - core, xh_], rb.at[xh_], sibling))

    wkv = wqkv_ref[:, D:]

    def scaled(v):
        v32 = v.astype(F32)
        return v32 * inverse_of(v32)

    def by_eight(v):
        return jnp.sum(v.reshape(HALF // 8, 8, D), axis=0)

    edge_l = mm(dproj[:HALF, D:], wkv, NT)
    esend[0] = edge_l.astype(BF16)
    e_moves = [push(esend.at[0], erecv.at[0], left)]
    edge_r = mm(dproj[2 * HALF:, D:], wkv, NT)
    esend[1] = edge_r.astype(BF16)
    e_moves.append(push(esend.at[1], erecv.at[1], right))

    for xh_ in range(2):
        member_grads(core, xh_)

    arrived(a_first)
    first_sums(sa, ga1, ha1, ga2, ha2)
    a_second = second_hops(ga2, ha2, ga3, ha3)

    arrived(b_core)
    core_sum(gb, rb, sb)
    b_first = first_hops(sb, gb1, hb1)

    arrived(u_z)
    total = u0[z].astype(F32)
    for o in range(NZ - 1):
        total = total + ruz[o].astype(F32)
    w0[...] = total
    u_core = [push(w0, ruc, sibling)]

    gain8 = by_eight(edge_l * scaled(xh[0])) + by_eight(edge_r * scaled(xh[1]))
    dnorm = mm(dproj[HALF:2 * HALF, :], wqkv_ref[...], NT)
    gain8 = gain8 + by_eight(dnorm * scaled(x_ref[...]))
    gain1 = jnp.sum(gain8, axis=0, keepdims=True)
    v0[...] = jnp.concatenate([gain1[:, i * 128:(i + 1) * 128] for i in range(4)] * 2, axis=0)
    v_core = [push(v0, vc, sibling)]

    arrived(u_core)
    rux[x] = w0[...] + ruc[...]
    u_x = [push(rux.at[x], rux.at[x], at(x_=v)) for v in xs]
    arrived(v_core)
    vx[x] = v0[...] + vc[...]
    v_x = [push(vx.at[x], vx.at[x], at(x_=v)) for v in xs]

    arrived(a_second)
    for i, value in enumerate(second_sums(ga2, ha2, ga3, ha3)):
        ga4[i] = value
    a_third = [push(ga4.at[v], ra4.at[o], at(z_=v)) for o, v in enumerate(zs)]

    arrived(b_first)
    first_sums(sb, gb1, hb1, gb2, hb2)
    b_second = second_hops(gb2, hb2, gb3, hb3)
    arrived(u_x)
    ruy[y] = rux[0] + rux[1] + rux[2] + rux[3]
    u_y = [push(ruy.at[y], ruy.at[y], at(y_=v)) for v in ys]
    arrived(v_x)
    vy[y] = vx[0] + vx[1] + vx[2] + vx[3]
    v_y = [push(vy.at[y], vy.at[y], at(y_=v)) for v in ys]

    arrived(e_moves)
    dnorm = dnorm + erecv[0].astype(F32) + erecv[1].astype(F32)
    x32 = x_ref[...].astype(F32)
    inverse = inverse_of(x32)
    dscaled = dnorm * gain
    dst_ref[...] = (
        dout[...].astype(F32)
        + inverse * dscaled
        - x32 * (inverse * inverse * inverse * jnp.mean(dscaled * x32, axis=-1, keepdims=True))
    ).astype(BF16)
    move(dst_ref, dst_hbm)

    arrived(b_second)
    for i, value in enumerate(second_sums(gb2, hb2, gb3, hb3)):
        gb4[i] = jnp.concatenate(
            [value[:, :HALF], jnp.concatenate([value[:, HALF:], value[:, HALF:]], axis=1)], axis=0
        ).astype(BF16)
    b_third = [push(gb4.at[v], rb4.at[o], at(z_=v)) for o, v in enumerate(zs)]
    arrived(u_y)
    fz[z] = (ruy[0] + ruy[1] + ruy[2] + ruy[3]).astype(BF16)
    f_z = [push(fz.at[z], fz.at[z], at(z_=v)) for v in zs]
    arrived(v_y)
    vz[z] = vy[0] + vy[1] + vy[2] + vy[3]
    v_z = [push(vz.at[z], vz.at[z], at(z_=v)) for v in zs]

    arrived(a_third)
    final = ga4[z]
    for o in range(NZ - 1):
        final = final + ra4[o]
    dwout_ref[...] = final
    arrived(b_third)
    final = gb4[z].astype(F32)
    for o in range(NZ - 1):
        final = final + rb4[o].astype(F32)
    dwqkv_ref[:, :HALF] = final[:8]
    dwqkv_ref[:, HALF:] = final[8:, :128]
    arrived(f_z)
    for i in range(NZ):
        value = fz[i].astype(F32)
        dbias_ref[i * 8:(i + 1) * 8, :HALF] = value[:8]
        dbias_ref[i * 8:(i + 1) * 8, HALF:] = value[8:]
    arrived(v_z)
    total = vz[0]
    for i in range(1, NZ):
        total = total + vz[i]
    for i in range(4):
        dgain_ref[:, i * 128:(i + 1) * 128] = total[i:i + 1]

    for c in started:
        c.wait_send()
    moves[-2].wait()
    moves[-1].wait()


def deliver(*refs):
    for i in range(5):
        refs[6 + i][...] = refs[i][...]
    refs[11][...] = refs[5][...].T


N_CHAIN = 6 + 6 + 7
N_COPIES = 2 + 2 + (1 + N_CHAIN) + (2 + N_CHAIN) + (7 + 1 + 3 + 3 + 7) + (1 + 3 + 3 + 7)


def scratch():
    def v(*shape, kind=BF16):
        return pltpu.VMEM(shape, kind)

    def chain(columns, last, kind):
        return [
            v(2, 2, 2, NXL, NY, 32, columns), v(2, 2, NXL, NY, 32, columns), v(2, NX, NY, 32, columns),
            v(NX - 1, NY, 32, columns), v(NY - 1, NX, 32, columns), v(NY, 32, columns), v(NX, 32, columns),
            v(NY - 1, 32, columns), v(NX - 1, 32, columns), v(NZ, *last, kind=kind), v(NZ - 1, *last, kind=kind),
        ]

    return [
        v(HALF, D), v(HALF, D), v(D, 3 * D), v(D, D), v(HEADS * PIX, PIX, kind=F32), v(HALF, D), v(HALF, D),
        v(2, HALF, D), v(3 * HALF, D), v(D, 3 * HALF), v(12, PIX, D), v(12, PIX, D), v(5, PIX, D, kind=F32),
        v(4, PIX, 128),
        v(HALF, D), v(ROWS, SLOTS * PIX, D), v(ROWS, SLOTS * PIX, D), v(ROWS, SLOTS * PIX, D, kind=F32),
        v(ROWS, SLOTS + 1, PIX, D), v(ROWS, 1, D, kind=F32), v(HALF, D), v(HALF, D), v(HALF, D),
        v(ROWS, SLOTS + 1, PIX, D), v(3 * HALF, 3 * D),
        v(2, ROWS * HALF, HALF), v(2, ROWS * HALF, HALF), v(2, 12 * PIX, ROWS * HALF), v(2, 12 * PIX, ROWS * HALF),
        v(2, HALF, D), v(2, HALF, D), v(SLOTS * PIX, 128),
        *chain(128, (8, 128), F32),
        *chain(384, (16, HALF), BF16),
        v(NZ, 16, HALF), v(NZ - 1, 16, HALF), v(16, HALF, kind=F32), v(16, HALF, kind=F32),
        v(NX, 16, HALF, kind=F32), v(NY, 16, HALF, kind=F32), v(NZ, 16, HALF),
        v(8, 128, kind=F32), v(8, 128, kind=F32), v(NX, 8, 128, kind=F32), v(NY, 8, 128, kind=F32),
        v(NZ, 8, 128, kind=F32),
        pltpu.SemaphoreType.DMA((N_COPIES,)), pltpu.SemaphoreType.DMA((N_COPIES,)), pltpu.SemaphoreType.DMA((7,)),
    ]


def shards(states, teacher, w_qkv, w_out, gain, bias, neighbours, valid, orient):
    vmem = pl.BlockSpec(memory_space=pltpu.VMEM)
    anywhere = pl.BlockSpec(memory_space=pl.ANY)
    smem = pl.BlockSpec(memory_space=pltpu.SMEM)
    shapes = [
        jax.ShapeDtypeStruct((HALF, D), BF16),
        jax.ShapeDtypeStruct((HALF, D), BF16),
        jax.ShapeDtypeStruct((8, 384), F32),
        jax.ShapeDtypeStruct((8, 128), F32),
        jax.ShapeDtypeStruct((1, D), F32),
        jax.ShapeDtypeStruct((PIX, D), F32),
    ]
    results = pl.pallas_call(
        kernel,
        out_shape=shapes,
        in_specs=[anywhere] * 4 + [vmem, anywhere] + [smem] * 3,
        out_specs=[anywhere] * 2 + [vmem] * 4,
        scratch_shapes=scratch(),
        compiler_params=pltpu.CompilerParams(
            collective_id=0, has_side_effects=True, vmem_limit_bytes=60 * 2**20
        ),
    )(
        states[0], teacher, w_qkv, w_out, gain.reshape(1, D), bias.reshape(HEADS * PIX, PIX),
        neighbours, valid, orient,
    )
    output, d_states, d_wqkv, d_wout, d_gain, d_bias = pl.pallas_call(
        deliver,
        out_shape=shapes[:5] + [jax.ShapeDtypeStruct((HEADS * PIX, PIX), F32)],
        in_specs=[vmem] * 6,
        out_specs=[vmem] * 6,
    )(*results)
    return output[None], d_states[None], d_wqkv, d_wout, d_gain[0], d_bias.reshape(HEADS, PIX, PIX)


def solution(mesh):
    return jax.shard_map(
        shards,
        mesh=mesh,
        in_specs=(
            P("member", "tile", None), P("tile", None), P(), P(), P(), P(),
            P("tile", None), P("tile", None), P("tile", None),
        ),
        out_specs=(
            P("member", "tile", None), P("member", "tile", None), P("tile", "member"), P("tile", "member"), P(), P(),
        ),
        check_vma=False,
    )
```

```python
import functools

import jax
import jax.numpy as jnp
from jax import lax
from jax.experimental import pallas as pl
from jax.experimental.pallas import tpu as pltpu
from jax.sharding import PartitionSpec as P

D = 512
HEADS = 8
HD = 64
PIX = 64
ROWS = 4
SLOTS = 9
HALF = 256
EPS = 1e-06
NEG = -1e30
MESH = pl.DeviceIdType.MESH
F32 = jnp.float32
BF16 = jnp.bfloat16

NX, NY, NZ, NXL = 4, 4, 8, 2
N_TILE = NXL * NY * NZ
SPLIT = 32

NN = (((1,), (0,)), ((), ()))
NT = (((1,), (1,)), ((), ()))
TN = (((0,), (0,)), ((), ()))


def mm(a, b, dims=NN):
    return lax.dot_general(a, b, dims, preferred_element_type=F32)


def kernel(
    x_hbm, teacher_hbm, wqkv_hbm, wout_hbm, gain_hbm, bias_hbm, near_hbm, valid_hbm, orient_hbm,
    out_hbm, dst_hbm, dwqkv_ref, dwout_ref, dgain_ref, dbias_ref,
    x_ref, teacher_ref, wqkv_ref, wout_ref, gain_ref, bias_ref, near_ref, valid_ref, orient_ref, out_ref, dst_ref,
    xh, nb, nbt, kbuf, vbuf, tb, oh, qb, kg, vg, sref, peak, pb, rinv, mixed, dmix, dout, dsb, dproj,
    qd, md, dcat, pcat, esend, erecv, turns,
    ga, ra, sa, ya, ga1, ha1, gb, rb, sb, yb, gb1, hb1, g2, h2, g3, h3, g4, r4,
    u0, ruz, w0, ruc, rux, ruy, fz, v0, vc, vx, vy, vz,
    send, recv, local,
):
    tile = lax.axis_index("tile")
    member = lax.axis_index("member")
    z = lax.rem(tile, NZ)
    y = lax.rem(tile // NZ, NY)
    x = (member // 2) * NXL + tile // (NZ * NY)
    core = lax.rem(member, 2)

    def at(x_=None, y_=None, z_=None, core_=None):
        x_ = x if x_ is None else x_
        y_ = y if y_ is None else y_
        z_ = z if z_ is None else z_
        core_ = core if core_ is None else core_
        return (lax.rem(x_, NXL) * NY + y_) * NZ + z_, (x_ // NXL) * 2 + core_

    right = (lax.rem(tile + 1, N_TILE), member)
    left = (lax.rem(tile + N_TILE - 1, N_TILE), member)
    sibling = at(core_=1 - core)
    xs = [lax.rem(x + o, NX) for o in range(1, NX)]
    ys = [lax.rem(y + o, NY) for o in range(1, NY)]
    zs = [lax.rem(z + o, NZ) for o in range(1, NZ)]
    peers = [left, right, sibling]
    peers += [at(x_=v) for v in xs] + [at(y_=v) for v in ys] + [at(z_=v) for v in zs]

    started = []
    moves = []

    def push(src, dst, to):
        n = len(started)
        copy = pltpu.make_async_remote_copy(
            src_ref=src, dst_ref=dst, send_sem=send.at[n], recv_sem=recv.at[n],
            device_id=to, device_id_type=MESH,
        )
        copy.start()
        started.append(copy)
        return copy

    def move(src, dst):
        copy = pltpu.make_async_copy(src, dst, local.at[len(moves)])
        copy.start()
        moves.append(copy)
        return copy

    left_over = []

    def all_sent():
        for c in started[len(left_over):]:
            c.wait_send()
            left_over.append(c)

    def arrived(copies):
        for c in copies:
            c.wait_recv()

    barrier = pltpu.get_barrier_semaphore()
    for p in peers:
        pl.semaphore_signal(barrier, inc=1, device_id=p, device_id_type=MESH)
    pl.semaphore_wait(barrier, len(peers))

    states_moves = [push(x_hbm, xh.at[0], right), push(x_hbm, xh.at[1], left)]

    load_x = move(x_hbm, x_ref)
    load_gain = move(gain_hbm, gain_ref)
    load_qkv = move(wqkv_hbm, wqkv_ref)
    load_bias = move(bias_hbm, bias_ref)
    load_tables = [move(near_hbm, near_ref), move(valid_hbm, valid_ref), move(orient_hbm, orient_ref)]
    load_out = move(wout_hbm, wout_ref)
    load_teacher = move(teacher_hbm, teacher_ref)

    load_gain.wait()
    gain = gain_ref[...]

    def inverse_of(v32):
        return lax.rsqrt(jnp.mean(v32 * v32, axis=-1, keepdims=True) + EPS)

    def normalise(m, v):
        v32 = v.astype(F32)
        low = (v32 * inverse_of(v32) * gain).astype(BF16)
        nb[m * HALF:(m + 1) * HALF, :] = low
        nbt[:, m * HALF:(m + 1) * HALF] = low.T

    load_x.wait()
    normalise(1, x_ref[...])
    own = nb[HALF:2 * HALF, :]
    load_qkv.wait()
    qb[...] = (mm(own, wqkv_ref[:, :D]).astype(BF16) * 0.125).astype(BF16)

    def keys_values(m):
        rows = nb[m * HALF:(m + 1) * HALF, :]
        kbuf[m * ROWS:(m + 1) * ROWS] = mm(rows, wqkv_ref[:, D:2 * D]).astype(BF16).reshape(ROWS, PIX, D)
        vbuf[m * ROWS:(m + 1) * ROWS] = mm(rows, wqkv_ref[:, 2 * D:]).astype(BF16).reshape(ROWS, PIX, D)

    keys_values(1)

    load_bias.wait()
    j = lax.broadcasted_iota(jnp.int32, (PIX, 128), 0)
    l = lax.broadcasted_iota(jnp.int32, (PIX, 128), 1)
    u, w = j // 8, j % 8
    for o in range(4):
        oh[o] = jnp.where(l == u * 8 + w, 1.0, 0.0).astype(BF16)
        pick = jnp.where(l[:, :PIX] == (u * 8 + w)[:, :PIX], 1.0, 0.0)
        tb[o] = lax.dot_general(
            pick, bias_ref[...], NT, precision=lax.Precision.HIGHEST, preferred_element_type=F32
        )
        u, w = w, 7 - u
    tb[4] = jnp.full((PIX, D), NEG, F32)

    head_row = lax.broadcasted_iota(jnp.int32, (HALF, HALF), 0) // HD
    head_lane = lax.broadcasted_iota(jnp.int32, (HALF, HALF), 1) // HD
    same_head = jnp.where(head_row == head_lane, 1.0, 0.0).astype(BF16)
    lane_head = lax.broadcasted_iota(jnp.int32, (PIX, HALF), 1) // HD

    def block_diagonal(v):
        return jnp.concatenate([v] * 4, axis=0) * same_head

    def diagonal(v):
        out = v[:PIX]
        for a in range(1, 4):
            out = jnp.where(lane_head == a, v[a * PIX:(a + 1) * PIX], out)
        return out

    groups = [slice(0, HALF), slice(HALF, D)]
    for c in load_tables:
        c.wait()
    tables = [[jnp.where(valid_ref[b, s] > 0, orient_ref[b, s], 4) for s in range(SLOTS)] for b in range(ROWS)]

    def score(b, slots, tops):
        for s in slots:
            at_block = (s // 3) * ROWS + lax.rem(near_ref[b, s], ROWS)
            kg[b, s * PIX:(s + 1) * PIX, :] = kbuf[at_block]
            vg[b, s * PIX:(s + 1) * PIX, :] = vbuf[at_block]
        first, n = slots[0], len(slots)
        for g, lanes in enumerate(groups):
            scores = mm(kg[b, first * PIX:(first + n) * PIX, lanes], qd[g, b * HALF:(b + 1) * HALF, :], NT)
            for i, s in enumerate(slots):
                piece = scores[i * PIX:(i + 1) * PIX] + tb[tables[b][s], :, lanes]
                sref[b, s * PIX:(s + 1) * PIX, lanes] = piece
                tops[g] = piece if tops[g] is None else jnp.maximum(tops[g], piece)

    for b in range(ROWS):
        for g, lanes in enumerate(groups):
            qd[g, b * HALF:(b + 1) * HALF, :] = block_diagonal(qb[b * PIX:(b + 1) * PIX, lanes])
        tops = [None, None]
        score(b, (3, 4, 5), tops)
        for g, lanes in enumerate(groups):
            peak[b, :, lanes] = tops[g]
        pb[b, SLOTS] = jnp.zeros((PIX, D), BF16)
        dsb[b, SLOTS] = jnp.zeros((PIX, D), BF16)
    dproj[:HALF, :D] = jnp.zeros((HALF, D), BF16)
    dproj[2 * HALF:, :D] = jnp.zeros((HALF, D), BF16)

    arrived(states_moves)
    normalise(0, xh[0])
    keys_values(0)
    normalise(2, xh[1])
    keys_values(2)

    for b in range(ROWS):
        tops = [peak[b, :, lanes] for lanes in groups]
        score(b, (0, 1, 2), tops)
        score(b, (6, 7, 8), tops)
        for g, lanes in enumerate(groups):
            top = jnp.max(tops[g], axis=0, keepdims=True)
            total = None
            for s in range(SLOTS):
                piece = jnp.exp(sref[b, s * PIX:(s + 1) * PIX, lanes] - top)
                sref[b, s * PIX:(s + 1) * PIX, lanes] = piece
                total = piece if total is None else total + piece
            share = 1.0 / jnp.sum(total, axis=0, keepdims=True)
            rinv[b, :, lanes] = share
            for s in range(SLOTS):
                piece = sref[b, s * PIX:(s + 1) * PIX, lanes] * share
                pb[b, s, :, lanes] = piece.astype(BF16)
            probs = pb[b, 0:SLOTS, :, lanes].reshape(SLOTS * PIX, HALF)
            mixed[b * PIX:(b + 1) * PIX, lanes] = diagonal(mm(probs, vg[b, :, lanes], TN)).astype(BF16)

    load_out.wait()
    load_teacher.wait()
    out32 = x_ref[...].astype(F32) + mm(mixed[...], wout_ref[...])
    out_ref[...] = out32.astype(BF16)
    move(out_ref, out_hbm)
    dout[...] = (out32 - teacher_ref[...].astype(F32)).astype(BF16)
    dmix[...] = mm(dout[...], wout_ref[...], NT).astype(BF16)

    def lay_out(grads, c, xh_, value):
        low = value.astype(BF16)
        for xl in range(NXL):
            for yy in range(NY):
                fb = xl * NY + yy
                grads[c, xh_, xl, yy] = low[fb * 64:(fb + 1) * 64]

    def core_sum(grads, got, one, two):
        for xh_ in range(2):
            for xl in range(NXL):
                total = (grads[core, xh_, xl].astype(F32) + got[xh_, xl].astype(F32)).astype(BF16)
                one[xh_ * NXL + xl] = total[:, :SPLIT]
                two[xh_ * NXL + xl] = total[:, SPLIT:]

    def first_hops(one, two, by_x, by_y):
        copies = [push(two.at[:, v], by_y.at[o], at(y_=v)) for o, v in enumerate(ys)]
        return copies + [push(one.at[v], by_x.at[o], at(x_=v)) for o, v in enumerate(xs)]

    def first_sums(one, two, by_x, by_y, lanes):
        g2[:, :, lanes] = (
            one[x].astype(F32) + by_x[0].astype(F32) + by_x[1].astype(F32) + by_x[2].astype(F32)
        ).astype(BF16)
        for xx in range(NX):
            h2[xx, :, lanes] = (
                two[xx, y].astype(F32) + by_y[0, xx].astype(F32) + by_y[1, xx].astype(F32)
                + by_y[2, xx].astype(F32)
            ).astype(BF16)

    grad_out = mm(mixed[...], dout[...], TN)
    for m in range(4):
        lay_out(ga, m % 2, m // 2, grad_out[:, m * 128:(m + 1) * 128])
    a_core = [push(ga.at[1 - core], ra, sibling)]

    dbias = None
    for b in range(ROWS):
        for g, lanes in enumerate(groups):
            diag = block_diagonal(dmix[b * PIX:(b + 1) * PIX, lanes])
            md[g, b * HALF:(b + 1) * HALF, :] = diag
            dprobs = mm(vg[b, :, lanes], diag, NT)
            share = rinv[b, :, lanes]
            total = None
            for s in range(SLOTS):
                piece = sref[b, s * PIX:(s + 1) * PIX, lanes] * dprobs[s * PIX:(s + 1) * PIX]
                total = piece if total is None else total + piece
            delta = jnp.sum(total, axis=0, keepdims=True) * share
            for s in range(SLOTS):
                piece = sref[b, s * PIX:(s + 1) * PIX, lanes] * share
                piece = piece * (dprobs[s * PIX:(s + 1) * PIX] - delta)
                dsb[b, s, :, lanes] = piece.astype(BF16)
            dscores = dsb[b, 0:SLOTS, :, lanes].reshape(SLOTS * PIX, HALF)
            dproj[HALF + b * PIX:HALF + (b + 1) * PIX, lanes] = (
                diagonal(mm(dscores, kg[b, :, lanes], TN)) * 0.125
            ).astype(BF16)
        for s in range(SLOTS):
            turns[s * PIX:(s + 1) * PIX, :] = oh[orient_ref[b, s]]
        term = mm(turns[...], dsb[b, 0:SLOTS].reshape(SLOTS * PIX, D), TN)[:PIX]
        dbias = term if dbias is None else dbias + term

    for i in range(NZ):
        u0[i] = jnp.concatenate(
            [dbias[i * 8:(i + 1) * 8, :HALF], dbias[i * 8:(i + 1) * 8, HALF:]], axis=0
        ).astype(BF16)
    u_z = [push(u0.at[v], ruz.at[o], at(z_=v)) for o, v in enumerate(zs)]

    arrived(a_core)
    core_sum(ga, ra, sa, ya)
    a_first = first_hops(sa, ya, ga1, ha1)

    for b in range(ROWS):
        rows = [lax.rem(near_ref[b, s], ROWS) for s in range(SLOTS)]
        for m in range(3):
            for t in range(ROWS):
                slots = [jnp.where(rows[3 * m + k] == t, 3 * m + k, SLOTS) for k in range(3)]
                here = slice((m * ROWS + t) * PIX, (m * ROWS + t + 1) * PIX)
                ds = dsb[b, slots[0]] + dsb[b, slots[1]] + dsb[b, slots[2]]
                ps = pb[b, slots[0]] + pb[b, slots[1]] + pb[b, slots[2]]
                for g, lanes in enumerate(groups):
                    dcat[g, here, b * HALF:(b + 1) * HALF] = ds[:, lanes]
                    pcat[g, here, b * HALF:(b + 1) * HALF] = ps[:, lanes]
    for g in range(2):
        dproj[:, D + g * HALF:D + (g + 1) * HALF] = mm(dcat[g], qd[g]).astype(BF16)
        dproj[:, 2 * D + g * HALF:2 * D + (g + 1) * HALF] = mm(pcat[g], md[g]).astype(BF16)

    wkv = wqkv_ref[:, D:]

    def scaled(v):
        v32 = v.astype(F32)
        return v32 * inverse_of(v32)

    def by_eight(v):
        return jnp.sum(v.reshape(HALF // 8, 8, D), axis=0)

    edge_l = mm(dproj[:HALF, D:], wkv, NT)
    esend[0] = edge_l.astype(BF16)
    e_moves = [push(esend.at[0], erecv.at[0], left)]
    edge_r = mm(dproj[2 * HALF:, D:], wkv, NT)
    esend[1] = edge_r.astype(BF16)
    e_moves.append(push(esend.at[1], erecv.at[1], right))

    def member_grads(c, xh_):
        lanes = pl.ds(pl.multiple_of((xh_ * 2 + c) * 384, 128), 384)
        lay_out(gb, c, xh_, mm(nbt[...], dproj[:, lanes]))

    b_core = []
    for xh_ in range(2):
        member_grads(1 - core, xh_)
        b_core.append(push(gb.at[1 - core, xh_], rb.at[xh_], sibling))

    arrived(u_z)
    total = u0[z].astype(F32)
    for o in range(NZ - 1):
        total = total + ruz[o].astype(F32)
    w0[...] = total
    u_core = [push(w0, ruc, sibling)]

    for xh_ in range(2):
        member_grads(core, xh_)

    arrived(a_first)
    first_sums(sa, ya, ga1, ha1, slice(384, D))

    arrived(u_core)
    rux[x] = w0[...] + ruc[...]
    u_x = [push(rux.at[x], rux.at[x], at(x_=v)) for v in xs]

    arrived(b_core)
    core_sum(gb, rb, sb, yb)
    b_first = first_hops(sb, yb, gb1, hb1)

    gain8 = by_eight(edge_l * scaled(xh[0])) + by_eight(edge_r * scaled(xh[1]))
    dnorm = mm(dproj[HALF:2 * HALF, :], wqkv_ref[...], NT)
    gain8 = gain8 + by_eight(dnorm * scaled(x_ref[...]))
    gain1 = jnp.sum(gain8, axis=0, keepdims=True)
    v0[...] = jnp.concatenate([gain1[:, i * 128:(i + 1) * 128] for i in range(4)] * 2, axis=0)
    v_core = [push(v0, vc, sibling)]

    arrived(u_x)
    ruy[y] = rux[0] + rux[1] + rux[2] + rux[3]
    u_y = [push(ruy.at[y], ruy.at[y], at(y_=v)) for v in ys]
    arrived(v_core)
    vx[x] = v0[...] + vc[...]
    v_x = [push(vx.at[x], vx.at[x], at(x_=v)) for v in xs]

    arrived(b_first)
    first_sums(sb, yb, gb1, hb1, slice(0, 384))
    second = [push(g2.at[v], g3.at[o], at(y_=v)) for o, v in enumerate(ys)]
    second += [push(h2.at[v], h3.at[o], at(x_=v)) for o, v in enumerate(xs)]
    arrived(u_y)
    fz[z] = (ruy[0] + ruy[1] + ruy[2] + ruy[3]).astype(BF16)
    f_z = [push(fz.at[z], fz.at[z], at(z_=v)) for v in zs]
    arrived(v_x)
    vy[y] = vx[0] + vx[1] + vx[2] + vx[3]
    v_y = [push(vy.at[y], vy.at[y], at(y_=v)) for v in ys]

    before = len(started) - len(second) - len(f_z) - len(v_y)
    for c in started[:before]:
        c.wait_send()
        left_over.append(c)

    arrived(e_moves)
    dnorm = dnorm + erecv[0].astype(F32) + erecv[1].astype(F32)
    x32 = x_ref[...].astype(F32)
    inverse = inverse_of(x32)
    dscaled = dnorm * gain
    dst_ref[...] = (
        dout[...].astype(F32)
        + inverse * dscaled
        - x32 * (inverse * inverse * inverse * jnp.mean(dscaled * x32, axis=-1, keepdims=True))
    ).astype(BF16)
    move(dst_ref, dst_hbm)

    arrived(second)
    ca = g2[y].astype(F32) + g3[0].astype(F32) + g3[1].astype(F32) + g3[2].astype(F32)
    cb = h2[x].astype(F32) + h3[0].astype(F32) + h3[1].astype(F32) + h3[2].astype(F32)
    for i in range(NZ):
        value = (ca if i < 4 else cb)[(i % 4) * 8:(i % 4) * 8 + 8]
        g4[i] = jnp.concatenate([value[:, :HALF], value[:, HALF:]], axis=0).astype(BF16)
    third = [push(g4.at[v], r4.at[o], at(z_=v)) for o, v in enumerate(zs)]
    arrived(v_y)
    vz[z] = vy[0] + vy[1] + vy[2] + vy[3]
    v_z = [push(vz.at[z], vz.at[z], at(z_=v)) for v in zs]

    arrived(third)
    final = g4[z].astype(F32)
    for o in range(NZ - 1):
        final = final + r4[o].astype(F32)
    dwqkv_ref[:, :HALF] = final[:8]
    dwqkv_ref[:, HALF:] = final[8:, :128]
    dwout_ref[...] = final[8:, 128:]
    arrived(f_z)
    for i in range(NZ):
        value = fz[i].astype(F32)
        dbias_ref[i * 8:(i + 1) * 8, :HALF] = value[:8]
        dbias_ref[i * 8:(i + 1) * 8, HALF:] = value[8:]
    arrived(v_z)
    total = vz[0]
    for i in range(1, NZ):
        total = total + vz[i]
    for i in range(4):
        dgain_ref[:, i * 128:(i + 1) * 128] = total[i:i + 1]

    all_sent()
    moves[-2].wait()
    moves[-1].wait()


def deliver(*refs):
    for i in range(5):
        refs[6 + i][...] = refs[i][...]
    refs[11][...] = refs[5][...].T


N_COPIES = 2 + 2 + (1 + 6) + (2 + 6) + 6 + 7 + (7 + 1 + 3 + 3 + 7) + (1 + 3 + 3 + 7)


def scratch():
    def v(*shape, kind=BF16):
        return pltpu.VMEM(shape, kind)

    def chain(columns):
        return [
            v(2, 2, NXL, NY, 64, columns), v(2, NXL, NY, 64, columns),
            v(NX, NY, SPLIT, columns), v(NX, NY, 64 - SPLIT, columns),
            v(NX - 1, NY, SPLIT, columns), v(NY - 1, NX, 64 - SPLIT, columns),
        ]

    return [
        v(HALF, D), v(HALF, D), v(D, 3 * D), v(D, D), v(1, D, kind=F32), v(HEADS * PIX, PIX, kind=F32),
        *[pltpu.SMEM((ROWS, SLOTS), jnp.int32)] * 3, v(HALF, D), v(HALF, D),
        v(2, HALF, D), v(3 * HALF, D), v(D, 3 * HALF), v(12, PIX, D), v(12, PIX, D), v(5, PIX, D, kind=F32),
        v(4, PIX, 128),
        v(HALF, D), v(ROWS, SLOTS * PIX, D), v(ROWS, SLOTS * PIX, D), v(ROWS, SLOTS * PIX, D, kind=F32),
        v(ROWS, PIX, D, kind=F32),
        v(ROWS, SLOTS + 1, PIX, D), v(ROWS, 1, D, kind=F32), v(HALF, D), v(HALF, D), v(HALF, D),
        v(ROWS, SLOTS + 1, PIX, D), v(3 * HALF, 3 * D),
        v(2, ROWS * HALF, HALF), v(2, ROWS * HALF, HALF), v(2, 12 * PIX, ROWS * HALF), v(2, 12 * PIX, ROWS * HALF),
        v(2, HALF, D), v(2, HALF, D), v(SLOTS * PIX, 128),
        *chain(128), *chain(384),
        v(NY, SPLIT, D), v(NX, 64 - SPLIT, D), v(NY - 1, SPLIT, D), v(NX - 1, 64 - SPLIT, D),
        v(NZ, 16, HALF), v(NZ - 1, 16, HALF),
        v(NZ, 16, HALF), v(NZ - 1, 16, HALF), v(16, HALF, kind=F32), v(16, HALF, kind=F32),
        v(NX, 16, HALF, kind=F32), v(NY, 16, HALF, kind=F32), v(NZ, 16, HALF),
        v(8, 128, kind=F32), v(8, 128, kind=F32), v(NX, 8, 128, kind=F32), v(NY, 8, 128, kind=F32),
        v(NZ, 8, 128, kind=F32),
        pltpu.SemaphoreType.DMA((N_COPIES,)), pltpu.SemaphoreType.DMA((N_COPIES,)), pltpu.SemaphoreType.DMA((11,)),
    ]


def shards(states, teacher, w_qkv, w_out, gain, bias, neighbours, valid, orient):
    vmem = pl.BlockSpec(memory_space=pltpu.VMEM)
    anywhere = pl.BlockSpec(memory_space=pl.ANY)
    shapes = [
        jax.ShapeDtypeStruct((HALF, D), BF16),
        jax.ShapeDtypeStruct((HALF, D), BF16),
        jax.ShapeDtypeStruct((8, 384), F32),
        jax.ShapeDtypeStruct((8, 128), F32),
        jax.ShapeDtypeStruct((1, D), F32),
        jax.ShapeDtypeStruct((PIX, D), F32),
    ]
    results = pl.pallas_call(
        kernel,
        out_shape=shapes,
        in_specs=[anywhere] * 9,
        out_specs=[anywhere] * 2 + [vmem] * 4,
        scratch_shapes=scratch(),
        compiler_params=pltpu.CompilerParams(
            collective_id=0, has_side_effects=True, vmem_limit_bytes=60 * 2**20
        ),
    )(
        states[0], teacher, w_qkv, w_out, gain.reshape(1, D), bias.reshape(HEADS * PIX, PIX),
        neighbours, valid, orient,
    )
    output, d_states, d_wqkv, d_wout, d_gain, d_bias = pl.pallas_call(
        deliver,
        out_shape=shapes[:5] + [jax.ShapeDtypeStruct((HEADS * PIX, PIX), F32)],
        in_specs=[vmem] * 6,
        out_specs=[vmem] * 6,
    )(*results)
    return output[None], d_states[None], d_wqkv, d_wout, d_gain[0], d_bias.reshape(HEADS, PIX, PIX)


def solution(mesh):
    return jax.shard_map(
        shards,
        mesh=mesh,
        in_specs=(
            P("member", "tile", None), P("tile", None), P(), P(), P(), P(),
            P("tile", None), P("tile", None), P("tile", None),
        ),
        out_specs=(
            P("member", "tile", None), P("member", "tile", None), P("tile", "member"), P("tile", "member"), P(), P(),
        ),
        check_vma=False,
    )
```

```python
import functools

import jax
import jax.numpy as jnp
from jax import lax
from jax.experimental import pallas as pl
from jax.experimental.pallas import tpu as pltpu
from jax.sharding import PartitionSpec as P

D = 512
HEADS = 8
HD = 64
PIX = 64
ROWS = 4
SLOTS = 9
HALF = 256
EPS = 1e-06
NEG = -1e30
MESH = pl.DeviceIdType.MESH
F32 = jnp.float32
BF16 = jnp.bfloat16

NX, NY, NZ, NXL = 4, 4, 8, 2
N_TILE = NXL * NY * NZ
SPLIT = 32

NN = (((1,), (0,)), ((), ()))
NT = (((1,), (1,)), ((), ()))
TN = (((0,), (0,)), ((), ()))


def mm(a, b, dims=NN):
    return lax.dot_general(a, b, dims, preferred_element_type=F32)


def kernel(
    x_hbm, teacher_hbm, wqkv_hbm, wout_hbm, gain_hbm, bias_hbm, near_hbm, valid_hbm, orient_hbm,
    out_hbm, dst_hbm, dwqkv_ref, dwout_ref, dgain_ref, dbias_ref,
    x_ref, teacher_ref, wqkv_ref, wout_ref, gain_ref, bias_ref, near_ref, valid_ref, orient_ref, out_ref, dst_ref,
    xh, nb, nbt, kbuf, vbuf, tb, oh, qb, kg, vg, sref, peak, pb, rinv, mixed, dmix, dout, dsb, dproj,
    qd, md, dcat, pcat, esend, erecv, turns,
    ga, ra, sa, ya, ga1, ha1, gb, rb, sb, yb, gb1, hb1, g2, h2, g3, h3, g4, r4,
    u0, ruz, w0, ruc, rux, ruy, fz, v0, vc, vx, vy, vz,
    send, recv, local,
):
    tile = lax.axis_index("tile")
    member = lax.axis_index("member")
    z = lax.rem(tile, NZ)
    y = lax.rem(tile // NZ, NY)
    x = (member // 2) * NXL + tile // (NZ * NY)
    core = lax.rem(member, 2)

    def at(x_=None, y_=None, z_=None, core_=None):
        x_ = x if x_ is None else x_
        y_ = y if y_ is None else y_
        z_ = z if z_ is None else z_
        core_ = core if core_ is None else core_
        return (lax.rem(x_, NXL) * NY + y_) * NZ + z_, (x_ // NXL) * 2 + core_

    right = (lax.rem(tile + 1, N_TILE), member)
    left = (lax.rem(tile + N_TILE - 1, N_TILE), member)
    sibling = at(core_=1 - core)
    xs = [lax.rem(x + o, NX) for o in range(1, NX)]
    ys = [lax.rem(y + o, NY) for o in range(1, NY)]
    zs = [lax.rem(z + o, NZ) for o in range(1, NZ)]
    peers = [left, right, sibling]
    peers += [at(x_=v) for v in xs] + [at(y_=v) for v in ys] + [at(z_=v) for v in zs]

    started = []
    moves = []

    def push(src, dst, to):
        n = len(started)
        copy = pltpu.make_async_remote_copy(
            src_ref=src, dst_ref=dst, send_sem=send.at[n], recv_sem=recv.at[n],
            device_id=to, device_id_type=MESH,
        )
        copy.start()
        started.append(copy)
        return copy

    def move(src, dst):
        copy = pltpu.make_async_copy(src, dst, local.at[len(moves)])
        copy.start()
        moves.append(copy)
        return copy

    left_over = []

    def all_sent():
        for c in started[len(left_over):]:
            c.wait_send()
            left_over.append(c)

    def arrived(copies):
        for c in copies:
            c.wait_recv()

    barrier = pltpu.get_barrier_semaphore()
    for p in peers:
        pl.semaphore_signal(barrier, inc=1, device_id=p, device_id_type=MESH)
    pl.semaphore_wait(barrier, len(peers))

    states_moves = [push(x_hbm, xh.at[0], right), push(x_hbm, xh.at[1], left)]

    load_x = move(x_hbm, x_ref)
    load_gain = move(gain_hbm, gain_ref)
    load_qkv = move(wqkv_hbm, wqkv_ref)
    load_bias = move(bias_hbm, bias_ref)
    load_tables = [move(near_hbm, near_ref), move(valid_hbm, valid_ref), move(orient_hbm, orient_ref)]
    load_out = move(wout_hbm, wout_ref)
    load_teacher = move(teacher_hbm, teacher_ref)

    load_gain.wait()
    gain = gain_ref[...]

    def inverse_of(v32):
        return lax.rsqrt(jnp.mean(v32 * v32, axis=-1, keepdims=True) + EPS)

    def normalise(m, v):
        v32 = v.astype(F32)
        low = (v32 * inverse_of(v32) * gain).astype(BF16)
        nb[m * HALF:(m + 1) * HALF, :] = low
        nbt[:, m * HALF:(m + 1) * HALF] = low.T

    load_x.wait()
    normalise(1, x_ref[...])
    own = nb[HALF:2 * HALF, :]
    load_qkv.wait()
    qb[...] = (mm(own, wqkv_ref[:, :D]).astype(BF16) * 0.125).astype(BF16)

    def keys_values(m):
        rows = nb[m * HALF:(m + 1) * HALF, :]
        kbuf[m * ROWS:(m + 1) * ROWS] = mm(rows, wqkv_ref[:, D:2 * D]).astype(BF16).reshape(ROWS, PIX, D)
        vbuf[m * ROWS:(m + 1) * ROWS] = mm(rows, wqkv_ref[:, 2 * D:]).astype(BF16).reshape(ROWS, PIX, D)

    keys_values(1)

    load_bias.wait()
    j = lax.broadcasted_iota(jnp.int32, (PIX, 128), 0)
    l = lax.broadcasted_iota(jnp.int32, (PIX, 128), 1)
    u, w = j // 8, j % 8
    for o in range(4):
        oh[o] = jnp.where(l == u * 8 + w, 1.0, 0.0).astype(BF16)
        pick = jnp.where(l[:, :PIX] == (u * 8 + w)[:, :PIX], 1.0, 0.0)
        tb[o] = lax.dot_general(
            pick, bias_ref[...], NT, precision=lax.Precision.HIGHEST, preferred_element_type=F32
        )
        u, w = w, 7 - u
    tb[4] = jnp.full((PIX, D), NEG, F32)

    head_row = lax.broadcasted_iota(jnp.int32, (HALF, HALF), 0) // HD
    head_lane = lax.broadcasted_iota(jnp.int32, (HALF, HALF), 1) // HD
    same_head = jnp.where(head_row == head_lane, 1.0, 0.0).astype(BF16)
    lane_head = lax.broadcasted_iota(jnp.int32, (PIX, HALF), 1) // HD

    def block_diagonal(v):
        return jnp.concatenate([v] * 4, axis=0) * same_head

    def diagonal(v):
        out = v[:PIX]
        for a in range(1, 4):
            out = jnp.where(lane_head == a, v[a * PIX:(a + 1) * PIX], out)
        return out

    groups = [slice(0, HALF), slice(HALF, D)]
    for c in load_tables:
        c.wait()
    tables = [[jnp.where(valid_ref[b, s] > 0, orient_ref[b, s], 4) for s in range(SLOTS)] for b in range(ROWS)]

    def score(b, slots, tops):
        for s in slots:
            at_block = (s // 3) * ROWS + lax.rem(near_ref[b, s], ROWS)
            kg[b, s * PIX:(s + 1) * PIX, :] = kbuf[at_block]
            vg[b, s * PIX:(s + 1) * PIX, :] = vbuf[at_block]
        first, n = slots[0], len(slots)
        for g, lanes in enumerate(groups):
            scores = mm(kg[b, first * PIX:(first + n) * PIX, lanes], qd[g, b * HALF:(b + 1) * HALF, :], NT)
            for i, s in enumerate(slots):
                piece = scores[i * PIX:(i + 1) * PIX] + tb[tables[b][s], :, lanes]
                sref[b, s * PIX:(s + 1) * PIX, lanes] = piece
                tops[g] = piece if tops[g] is None else jnp.maximum(tops[g], piece)

    for b in range(ROWS):
        for g, lanes in enumerate(groups):
            qd[g, b * HALF:(b + 1) * HALF, :] = block_diagonal(qb[b * PIX:(b + 1) * PIX, lanes])
        tops = [None, None]
        score(b, (3, 4, 5), tops)
        for g, lanes in enumerate(groups):
            peak[b, :, lanes] = tops[g]
        pb[b, SLOTS] = jnp.zeros((PIX, D), BF16)
        dsb[b, SLOTS] = jnp.zeros((PIX, D), BF16)
    dproj[:HALF, :D] = jnp.zeros((HALF, D), BF16)
    dproj[2 * HALF:, :D] = jnp.zeros((HALF, D), BF16)

    arrived(states_moves)
    normalise(0, xh[0])
    keys_values(0)
    normalise(2, xh[1])
    keys_values(2)

    def column(row):
        return jnp.broadcast_to(row, (8, HALF)).T[:, :1]

    for b in range(ROWS):
        tops = [peak[b, :, lanes] for lanes in groups]
        score(b, (0, 1, 2), tops)
        score(b, (6, 7, 8), tops)
        for g, lanes in enumerate(groups):
            top = jnp.max(tops[g], axis=0, keepdims=True)
            total = None
            for s in range(SLOTS):
                piece = jnp.exp(sref[b, s * PIX:(s + 1) * PIX, lanes] - top)
                sref[b, s * PIX:(s + 1) * PIX, lanes] = piece
                pb[b, s, :, lanes] = piece.astype(BF16)
                total = piece if total is None else total + piece
            share = 1.0 / jnp.sum(total, axis=0, keepdims=True)
            rinv[b, :, lanes] = share
            probs = pb[b, 0:SLOTS, :, lanes].reshape(SLOTS * PIX, HALF)
            mixed[b * PIX:(b + 1) * PIX, lanes] = diagonal(
                mm(probs, vg[b, :, lanes], TN) * column(share)
            ).astype(BF16)

    load_out.wait()
    load_teacher.wait()
    out32 = x_ref[...].astype(F32) + mm(mixed[...], wout_ref[...])
    out_ref[...] = out32.astype(BF16)
    move(out_ref, out_hbm)
    dout[...] = (out32 - teacher_ref[...].astype(F32)).astype(BF16)
    dmix[...] = mm(dout[...], wout_ref[...], NT).astype(BF16)

    def lay_out(grads, c, xh_, value):
        low = value.astype(BF16)
        for xl in range(NXL):
            for yy in range(NY):
                fb = xl * NY + yy
                grads[c, xh_, xl, yy] = low[fb * 64:(fb + 1) * 64]

    def core_sum(grads, got, one, two):
        for xh_ in range(2):
            for xl in range(NXL):
                total = (grads[core, xh_, xl].astype(F32) + got[xh_, xl].astype(F32)).astype(BF16)
                one[xh_ * NXL + xl] = total[:, :SPLIT]
                two[xh_ * NXL + xl] = total[:, SPLIT:]

    def first_hops(one, two, by_x, by_y):
        copies = [push(two.at[:, v], by_y.at[o], at(y_=v)) for o, v in enumerate(ys)]
        return copies + [push(one.at[v], by_x.at[o], at(x_=v)) for o, v in enumerate(xs)]

    def first_sums(one, two, by_x, by_y, lanes):
        g2[:, :, lanes] = (
            one[x].astype(F32) + by_x[0].astype(F32) + by_x[1].astype(F32) + by_x[2].astype(F32)
        ).astype(BF16)
        for xx in range(NX):
            h2[xx, :, lanes] = (
                two[xx, y].astype(F32) + by_y[0, xx].astype(F32) + by_y[1, xx].astype(F32)
                + by_y[2, xx].astype(F32)
            ).astype(BF16)

    grad_out = mm(mixed[...], dout[...], TN)
    for m in range(4):
        lay_out(ga, m % 2, m // 2, grad_out[:, m * 128:(m + 1) * 128])
    a_core = [push(ga.at[1 - core], ra, sibling)]

    dbias = None
    for b in range(ROWS):
        for g, lanes in enumerate(groups):
            share = rinv[b, :, lanes]
            rows = jnp.concatenate([dmix[b * PIX:(b + 1) * PIX, lanes].astype(F32)] * 4, axis=0)
            diag = (rows * column(share)).astype(BF16) * same_head
            md[g, b * HALF:(b + 1) * HALF, :] = diag
            dprobs = mm(vg[b, :, lanes], diag, NT)
            total = None
            for s in range(SLOTS):
                piece = sref[b, s * PIX:(s + 1) * PIX, lanes] * dprobs[s * PIX:(s + 1) * PIX]
                total = piece if total is None else total + piece
            delta = jnp.sum(total, axis=0, keepdims=True) * share
            for s in range(SLOTS):
                piece = sref[b, s * PIX:(s + 1) * PIX, lanes] * (dprobs[s * PIX:(s + 1) * PIX] - delta)
                dsb[b, s, :, lanes] = piece.astype(BF16)
            dscores = dsb[b, 0:SLOTS, :, lanes].reshape(SLOTS * PIX, HALF)
            dproj[HALF + b * PIX:HALF + (b + 1) * PIX, lanes] = (
                diagonal(mm(dscores, kg[b, :, lanes], TN)) * 0.125
            ).astype(BF16)
        for s in range(SLOTS):
            turns[s * PIX:(s + 1) * PIX, :] = oh[orient_ref[b, s]]
        term = mm(turns[...], dsb[b, 0:SLOTS].reshape(SLOTS * PIX, D), TN)[:PIX]
        dbias = term if dbias is None else dbias + term

    for i in range(NZ):
        u0[i] = jnp.concatenate(
            [dbias[i * 8:(i + 1) * 8, :HALF], dbias[i * 8:(i + 1) * 8, HALF:]], axis=0
        ).astype(BF16)
    u_z = [push(u0.at[v], ruz.at[o], at(z_=v)) for o, v in enumerate(zs)]

    arrived(a_core)
    core_sum(ga, ra, sa, ya)
    a_first = first_hops(sa, ya, ga1, ha1)

    for b in range(ROWS):
        rows = [lax.rem(near_ref[b, s], ROWS) for s in range(SLOTS)]
        for m in range(3):
            for t in range(ROWS):
                slots = [jnp.where(rows[3 * m + k] == t, 3 * m + k, SLOTS) for k in range(3)]
                here = slice((m * ROWS + t) * PIX, (m * ROWS + t + 1) * PIX)
                ds = dsb[b, slots[0]] + dsb[b, slots[1]] + dsb[b, slots[2]]
                ps = pb[b, slots[0]] + pb[b, slots[1]] + pb[b, slots[2]]
                for g, lanes in enumerate(groups):
                    dcat[g, here, b * HALF:(b + 1) * HALF] = ds[:, lanes]
                    pcat[g, here, b * HALF:(b + 1) * HALF] = ps[:, lanes]
    for g in range(2):
        dproj[:, D + g * HALF:D + (g + 1) * HALF] = mm(dcat[g], qd[g]).astype(BF16)
        dproj[:, 2 * D + g * HALF:2 * D + (g + 1) * HALF] = mm(pcat[g], md[g]).astype(BF16)

    wkv = wqkv_ref[:, D:]

    def scaled(v):
        v32 = v.astype(F32)
        return v32 * inverse_of(v32)

    def by_eight(v):
        return jnp.sum(v.reshape(HALF // 8, 8, D), axis=0)

    edge_l = mm(dproj[:HALF, D:], wkv, NT)
    esend[0] = edge_l.astype(BF16)
    e_moves = [push(esend.at[0], erecv.at[0], left)]
    edge_r = mm(dproj[2 * HALF:, D:], wkv, NT)
    esend[1] = edge_r.astype(BF16)
    e_moves.append(push(esend.at[1], erecv.at[1], right))

    def member_grads(c, xh_):
        lanes = pl.ds(pl.multiple_of((xh_ * 2 + c) * 384, 128), 384)
        lay_out(gb, c, xh_, mm(nbt[...], dproj[:, lanes]))

    b_core = []
    for xh_ in range(2):
        member_grads(1 - core, xh_)
        b_core.append(push(gb.at[1 - core, xh_], rb.at[xh_], sibling))

    arrived(u_z)
    total = u0[z].astype(F32)
    for o in range(NZ - 1):
        total = total + ruz[o].astype(F32)
    w0[...] = total
    u_core = [push(w0, ruc, sibling)]

    for xh_ in range(2):
        member_grads(core, xh_)

    arrived(a_first)
    first_sums(sa, ya, ga1, ha1, slice(384, D))

    arrived(u_core)
    rux[x] = w0[...] + ruc[...]
    u_x = [push(rux.at[x], rux.at[x], at(x_=v)) for v in xs]

    arrived(b_core)
    core_sum(gb, rb, sb, yb)
    b_first = first_hops(sb, yb, gb1, hb1)

    gain8 = by_eight(edge_l * scaled(xh[0])) + by_eight(edge_r * scaled(xh[1]))
    dnorm = mm(dproj[HALF:2 * HALF, :], wqkv_ref[...], NT)
    gain8 = gain8 + by_eight(dnorm * scaled(x_ref[...]))
    gain1 = jnp.sum(gain8, axis=0, keepdims=True)
    v0[...] = jnp.concatenate([gain1[:, i * 128:(i + 1) * 128] for i in range(4)] * 2, axis=0)
    v_core = [push(v0, vc, sibling)]

    arrived(u_x)
    ruy[y] = rux[0] + rux[1] + rux[2] + rux[3]
    u_y = [push(ruy.at[y], ruy.at[y], at(y_=v)) for v in ys]
    arrived(v_core)
    vx[x] = v0[...] + vc[...]
    v_x = [push(vx.at[x], vx.at[x], at(x_=v)) for v in xs]

    arrived(b_first)
    first_sums(sb, yb, gb1, hb1, slice(0, 384))
    second = [push(g2.at[v], g3.at[o], at(y_=v)) for o, v in enumerate(ys)]
    second += [push(h2.at[v], h3.at[o], at(x_=v)) for o, v in enumerate(xs)]
    arrived(u_y)
    fz[z] = (ruy[0] + ruy[1] + ruy[2] + ruy[3]).astype(BF16)
    f_z = [push(fz.at[z], fz.at[z], at(z_=v)) for v in zs]
    arrived(v_x)
    vy[y] = vx[0] + vx[1] + vx[2] + vx[3]
    v_y = [push(vy.at[y], vy.at[y], at(y_=v)) for v in ys]

    before = len(started) - len(second) - len(f_z) - len(v_y)
    for c in started[:before]:
        c.wait_send()
        left_over.append(c)

    arrived(e_moves)
    dnorm = dnorm + erecv[0].astype(F32) + erecv[1].astype(F32)
    x32 = x_ref[...].astype(F32)
    inverse = inverse_of(x32)
    dscaled = dnorm * gain
    dst_ref[...] = (
        dout[...].astype(F32)
        + inverse * dscaled
        - x32 * (inverse * inverse * inverse * jnp.mean(dscaled * x32, axis=-1, keepdims=True))
    ).astype(BF16)
    move(dst_ref, dst_hbm)

    arrived(second)
    ca = g2[y].astype(F32) + g3[0].astype(F32) + g3[1].astype(F32) + g3[2].astype(F32)
    cb = h2[x].astype(F32) + h3[0].astype(F32) + h3[1].astype(F32) + h3[2].astype(F32)
    for i in range(NZ):
        value = (ca if i < 4 else cb)[(i % 4) * 8:(i % 4) * 8 + 8]
        g4[i] = jnp.concatenate([value[:, :HALF], value[:, HALF:]], axis=0).astype(BF16)
    third = [push(g4.at[v], r4.at[o], at(z_=v)) for o, v in enumerate(zs)]
    arrived(v_y)
    vz[z] = vy[0] + vy[1] + vy[2] + vy[3]
    v_z = [push(vz.at[z], vz.at[z], at(z_=v)) for v in zs]

    arrived(third)
    final = g4[z].astype(F32)
    for o in range(NZ - 1):
        final = final + r4[o].astype(F32)
    dwqkv_ref[:, :HALF] = final[:8]
    dwqkv_ref[:, HALF:] = final[8:, :128]
    dwout_ref[...] = final[8:, 128:]
    arrived(f_z)
    for i in range(NZ):
        value = fz[i].astype(F32)
        dbias_ref[i * 8:(i + 1) * 8, :HALF] = value[:8]
        dbias_ref[i * 8:(i + 1) * 8, HALF:] = value[8:]
    arrived(v_z)
    total = vz[0]
    for i in range(1, NZ):
        total = total + vz[i]
    for i in range(4):
        dgain_ref[:, i * 128:(i + 1) * 128] = total[i:i + 1]

    all_sent()
    moves[-2].wait()
    moves[-1].wait()


def deliver(*refs):
    for i in range(5):
        refs[6 + i][...] = refs[i][...]
    refs[11][...] = refs[5][...].T


N_COPIES = 2 + 2 + (1 + 6) + (2 + 6) + 6 + 7 + (7 + 1 + 3 + 3 + 7) + (1 + 3 + 3 + 7)


def scratch():
    def v(*shape, kind=BF16):
        return pltpu.VMEM(shape, kind)

    def chain(columns):
        return [
            v(2, 2, NXL, NY, 64, columns), v(2, NXL, NY, 64, columns),
            v(NX, NY, SPLIT, columns), v(NX, NY, 64 - SPLIT, columns),
            v(NX - 1, NY, SPLIT, columns), v(NY - 1, NX, 64 - SPLIT, columns),
        ]

    return [
        v(HALF, D), v(HALF, D), v(D, 3 * D), v(D, D), v(1, D, kind=F32), v(HEADS * PIX, PIX, kind=F32),
        *[pltpu.SMEM((ROWS, SLOTS), jnp.int32)] * 3, v(HALF, D), v(HALF, D),
        v(2, HALF, D), v(3 * HALF, D), v(D, 3 * HALF), v(12, PIX, D), v(12, PIX, D), v(5, PIX, D, kind=F32),
        v(4, PIX, 128),
        v(HALF, D), v(ROWS, SLOTS * PIX, D), v(ROWS, SLOTS * PIX, D), v(ROWS, SLOTS * PIX, D, kind=F32),
        v(ROWS, PIX, D, kind=F32),
        v(ROWS, SLOTS + 1, PIX, D), v(ROWS, 1, D, kind=F32), v(HALF, D), v(HALF, D), v(HALF, D),
        v(ROWS, SLOTS + 1, PIX, D), v(3 * HALF, 3 * D),
        v(2, ROWS * HALF, HALF), v(2, ROWS * HALF, HALF), v(2, 12 * PIX, ROWS * HALF), v(2, 12 * PIX, ROWS * HALF),
        v(2, HALF, D), v(2, HALF, D), v(SLOTS * PIX, 128),
        *chain(128), *chain(384),
        v(NY, SPLIT, D), v(NX, 64 - SPLIT, D), v(NY - 1, SPLIT, D), v(NX - 1, 64 - SPLIT, D),
        v(NZ, 16, HALF), v(NZ - 1, 16, HALF),
        v(NZ, 16, HALF), v(NZ - 1, 16, HALF), v(16, HALF, kind=F32), v(16, HALF, kind=F32),
        v(NX, 16, HALF, kind=F32), v(NY, 16, HALF, kind=F32), v(NZ, 16, HALF),
        v(8, 128, kind=F32), v(8, 128, kind=F32), v(NX, 8, 128, kind=F32), v(NY, 8, 128, kind=F32),
        v(NZ, 8, 128, kind=F32),
        pltpu.SemaphoreType.DMA((N_COPIES,)), pltpu.SemaphoreType.DMA((N_COPIES,)), pltpu.SemaphoreType.DMA((11,)),
    ]


def shards(states, teacher, w_qkv, w_out, gain, bias, neighbours, valid, orient):
    vmem = pl.BlockSpec(memory_space=pltpu.VMEM)
    anywhere = pl.BlockSpec(memory_space=pl.ANY)
    shapes = [
        jax.ShapeDtypeStruct((HALF, D), BF16),
        jax.ShapeDtypeStruct((HALF, D), BF16),
        jax.ShapeDtypeStruct((8, 384), F32),
        jax.ShapeDtypeStruct((8, 128), F32),
        jax.ShapeDtypeStruct((1, D), F32),
        jax.ShapeDtypeStruct((PIX, D), F32),
    ]
    results = pl.pallas_call(
        kernel,
        out_shape=shapes,
        in_specs=[anywhere] * 9,
        out_specs=[anywhere] * 2 + [vmem] * 4,
        scratch_shapes=scratch(),
        compiler_params=pltpu.CompilerParams(
            collective_id=0, has_side_effects=True, vmem_limit_bytes=60 * 2**20
        ),
    )(
        states[0], teacher, w_qkv, w_out, gain.reshape(1, D), bias.reshape(HEADS * PIX, PIX),
        neighbours, valid, orient,
    )
    output, d_states, d_wqkv, d_wout, d_gain, d_bias = pl.pallas_call(
        deliver,
        out_shape=shapes[:5] + [jax.ShapeDtypeStruct((HEADS * PIX, PIX), F32)],
        in_specs=[vmem] * 6,
        out_specs=[vmem] * 6,
    )(*results)
    return output[None], d_states[None], d_wqkv, d_wout, d_gain[0], d_bias.reshape(HEADS, PIX, PIX)


def solution(mesh):
    return jax.shard_map(
        shards,
        mesh=mesh,
        in_specs=(
            P("member", "tile", None), P("tile", None), P(), P(), P(), P(),
            P("tile", None), P("tile", None), P("tile", None),
        ),
        out_specs=(
            P("member", "tile", None), P("member", "tile", None), P("tile", "member"), P("tile", "member"), P(), P(),
        ),
        check_vma=False,
    )
```
